128 devices in a mesh: dp: 16 (over x, z), expert: 8 (over y, core).
Axes of the slice: x: 4, y: 4, z: 4, core: 2. Of those that a mesh axis runs over, the one named last changes fastest.
Arguments:
- tokens: bfloat16 [4096, 8192], P('dp', 'expert'), may hold values from -6 to 6
- w_in: bfloat16 [8192, 32768], P('expert', 'dp'), may hold values from -0.0625 to 0.0625
- w_out: bfloat16 [32768, 8192], P('dp', 'expert'), may hold values from -0.03125 to 0.03125
- chosen: int32 [16, 64], P('dp'), may hold values from 0 to 255, as said below
- counts: int32 [16], P('dp'), may hold values from 1 to 64, 512 in all
- gates: float32 [16, 64], P('dp'), may hold values from 0.1 to 1
- cotangent: bfloat16 [4096, 8192], P('dp', 'expert'), may hold values from -6 to 6
Outputs:
- mixed: bfloat16 [4096, 8192], P('dp', 'expert')
- d_tokens: bfloat16 [4096, 8192], P('dp', 'expert')
- d_w_in: bfloat16 [8192, 32768], P('expert', 'dp')
- d_w_out: bfloat16 [32768, 8192], P('dp', 'expert')
The draws below stay inside these ranges and needn't reach their ends.
Inputs may be any that keep to these rules, and one draw needn't show every extreme that they name: `chosen`: row i lists local indices of tokens of shard i; its first counts[i] entries name the tokens the expert chose there and are distinct; the other entries are ignored. `counts`: entry i is the number of used entries of row i of chosen; the entries sum to exactly 512, and some shard has exactly 64.
All inputs are finite; a program needn't handle non-finite values.
Results may differ from the reference program's by a relative error of at most 0.029.
Values may be sent and summed in bfloat16 or wider, within the bound.
A program may use at most 128 MiB of HBM per device.

```python
import math
import jax
import jax.numpy as jnp
import numpy as np
from jax import lax

D = 8192
F = 32768
SLOT = 64
TOK_DEV = 256
TOKENS = 4096
CAP = 512
DBLK = 1024
N_DP = 16


def draw_chosen(key, part):
    key = jax.random.fold_in(key, 11)
    row_keys = jax.random.split(key, N_DP)

    def one_row(row_key):
        return jax.random.permutation(row_key, TOK_DEV)[:SLOT]
    return jax.vmap(one_row)(row_keys).astype(jnp.int32)


def shard_levels(key, extent, pieces, least, high):
    loudness, own = 1.0, jax.random.fold_in(key, 6)
    for position, shards_of in pieces:
        draws = jnp.exp(jax.random.uniform(jax.random.fold_in(own, position), (shards_of,), jnp.float32, least / len(pieces), high / len(pieces)))
        loudness = loudness * jnp.repeat(draws, extent[position] // shards_of).reshape([-1 if axis == position else 1 for axis in range(len(extent))])
    return loudness


def profile(count, total, reach, skew):
    loads = [(1 << 20) // math.isqrt(rank ** skew) + 1 for rank in range(2, count + 1)]
    rest, holding = total - reach - (count - 1), [1] * (count - 1)
    while rest > 0:
        free = [i for i in range(count - 1) if holding[i] < reach]
        whole, remaining = sum([loads[i] for i in free]), rest
        for i in free:
            addition = min(reach - holding[i], max(1, remaining * loads[i] // whole), rest)
            holding[i] = holding[i] + addition
            rest = rest - addition
    return np.array([reach] + holding)


def ragged_sizes(stream_key, amount, total, most, slope):
    if amount == 2:
        one = jax.random.randint(stream_key, (), max(1, total - most), min(most, total - 1) + 1)
        return jnp.stack([one, total - one])
    sizes = jnp.asarray(profile(amount, total, most, slope), jnp.int32)
    pairs = (amount - 1) // 2
    source_of, sink = sizes[1:1 + 2 * pairs:2], sizes[2:2 + 2 * pairs:2]
    slack = jnp.minimum(source_of - 1, most - sink)
    moved = jax.random.randint(jax.random.fold_in(stream_key, 1), (pairs,), 0, 1 << 20) % (slack + 1)
    sizes = sizes.at[1:1 + 2 * pairs:2].set(source_of - moved).at[2:2 + 2 * pairs:2].set(sink + moved)
    return sizes[jax.random.permutation(jax.random.fold_in(stream_key, 2), amount)]


def scatter_about(key, shape, scale, limit, cuts=(), kind=jnp.bfloat16):
    drawn = jax.random.normal(key, shape, jnp.float32) * scale
    if len(cuts) > 0:
        drawn = shard_levels(key, shape, cuts, -0.22, 0.18) * drawn
    return jnp.clip(drawn, min=-limit, max=limit).astype(kind)


def setup_inputs(seed: int = 0) -> dict:
    key_of = jax.random.split(jax.random.key(seed), 8)
    return {
        "tokens": scatter_about(key_of[0], (TOKENS, D), 1.0, 6.0, ((0, 16), (1, 8))),
        "w_in": scatter_about(key_of[1], (D, F), D ** -0.5, 0.0625, ((0, 8), (1, 16))),
        "w_out": scatter_about(key_of[2], (F, D), F ** -0.5, 0.03125, ((0, 16), (1, 8))),
        "chosen": draw_chosen(jax.random.fold_in(key_of[7], 71), 0),
        "counts": ragged_sizes(key_of[4], N_DP, CAP, SLOT, 2).astype(jnp.int32),
        "gates": jnp.clip(jnp.exp(math.log(1.0) - 2.3025851 * jax.random.uniform(key_of[5], (N_DP, SLOT), jnp.float32) ** shard_levels(key_of[5], (N_DP, SLOT), ((0, 16),), -0.2, 0.2)), 0.1, 1.0),
        "cotangent": scatter_about(key_of[6], (TOKENS, D), 1.0, 6.0, ((0, 16), (1, 8))),
    }


half_root = 0.7071067811865476
inv_root_tau = 0.3989422804014327


def gelu_pair(pre_act):
    cdf_part = 0.5 * (1.0 + lax.erf(pre_act * half_root))
    slopes = cdf_part + pre_act * jnp.exp(-0.5 * pre_act * pre_act) * inv_root_tau
    return pre_act * cdf_part, slopes


def block_sum(left_side, right_side, right_axis, width_out):
    blocks = D // DBLK

    def add_block(block_index, summed):
        first = block_index * DBLK
        left_part = lax.dynamic_slice_in_dim(left_side, first, DBLK, 1)
        right_part = lax.dynamic_slice_in_dim(right_side, first, DBLK, right_axis)
        product = lax.dot_general(left_part, right_part, (((1,), (right_axis,)), ((), ())), preferred_element_type=jnp.float32)
        rounded = lax.optimization_barrier(product.astype(jnp.bfloat16))
        return summed + rounded.astype(jnp.float32)

    start_sum = jnp.zeros((left_side.shape[0], width_out), jnp.float32)
    return lax.fori_loop(0, blocks, add_block, start_sum)


def reference(tokens, w_in, w_out, chosen, counts, gates, cotangent):
    shards = chosen.shape[0]
    slot_count = chosen.shape[1]
    slot_range = jnp.arange(slot_count).astype(jnp.int32)
    live_mask = slot_range[None, :] < counts[:, None]
    starts = (jnp.cumsum(counts) - counts).astype(jnp.int32)
    slot_spot = jnp.where(live_mask, starts[:, None] + slot_range[None, :], CAP).astype(jnp.int32).reshape(-1)
    source = (jnp.arange(shards).astype(jnp.int32)[:, None] * TOK_DEV + chosen).astype(jnp.int32).reshape(-1)
    rows_of = jnp.zeros((CAP,), jnp.int32).at[slot_spot].set(source, mode="drop")
    gate_of = jnp.zeros((CAP,), jnp.float32).at[slot_spot].set(gates.reshape(-1).astype(jnp.float32), mode="drop")
    chosen_rows = tokens[rows_of]
    grad_rows = (gate_of[:, None] * cotangent[rows_of].astype(jnp.float32)).astype(jnp.bfloat16)
    pre_act = block_sum(chosen_rows, w_in, 0, F)
    activated, slopes = gelu_pair(pre_act)
    hidden = activated.astype(jnp.bfloat16)
    expert_out = jnp.dot(hidden, w_out, preferred_element_type=jnp.float32)
    mixed = jnp.zeros((TOKENS, D), jnp.float32).at[rows_of].add(gate_of[:, None] * expert_out).astype(jnp.bfloat16)
    back_hidden = block_sum(grad_rows, w_out, 1, F)
    back_pre = (back_hidden * slopes).astype(jnp.bfloat16)
    d_w_out = lax.dot_general(hidden, grad_rows, (((0,), (0,)), ((), ())), preferred_element_type=jnp.float32).astype(jnp.bfloat16)
    d_w_in = lax.dot_general(chosen_rows, back_pre, (((0,), (0,)), ((), ())), preferred_element_type=jnp.float32).astype(jnp.bfloat16)
    d_rows = lax.dot_general(back_pre, w_in, (((1,), (1,)), ((), ())), preferred_element_type=jnp.float32)
    d_tokens = jnp.zeros((TOKENS, D), jnp.float32).at[rows_of].add(d_rows).astype(jnp.bfloat16)
    return (mixed, d_tokens, d_w_in, d_w_out)
```

```python
import jax
import jax.numpy as jnp
from jax import lax
from jax.experimental import pallas as pl
from jax.experimental.pallas import tpu as pltpu
from jax.sharding import PartitionSpec as P

half_root = 0.7071067811865476
inv_root_tau = 0.3989422804014327

MESH = pl.DeviceIdType.MESH
BF = jnp.bfloat16
F32 = jnp.float32

N_COPIES = 240
N_LOCAL = 16

NN = (((1,), (0,)), ((), ()))
NT = (((1,), (1,)), ((), ()))


def dot(a, b, dims=NN):
    return lax.dot_general(a, b, dims, preferred_element_type=F32)


def gelu_pair(pre_act):
    cdf_part = 0.5 * (1.0 + lax.erf(pre_act * half_root))
    slopes = cdf_part + pre_act * jnp.exp(-0.5 * pre_act * pre_act) * inv_root_tau
    return (pre_act * cdf_part, slopes)


def wrap(v):
    return lax.rem(v + 8, 4)


def kernel(
    pick_ref, gate_ref, count_ref, tok_hbm, cot_hbm, wi_hbm, wo_hbm,
    rows_out, hb_out, slots_out,
    tok, cot, wi, wo, ag, cnt, c_mat, ct, rows, xs, xr, ps, opp_rx, nbr_rx, acc, slope, hb,
    part, spread, f_opp, f_nbr, grouped, s_opp, s_nbr,
    send_sem, recv_sem, local_sem,
):
    dp, ex = lax.axis_index("dp"), lax.axis_index("expert")
    x, z = lax.div(dp, 4), lax.rem(dp, 4)
    y, c = lax.div(ex, 2), lax.rem(ex, 2)
    oc = 1 - c
    dev_x = {1: (wrap(x + 1) * 4 + z, ex), -1: (wrap(x - 1) * 4 + z, ex)}
    dev_z = {1: (x * 4 + wrap(z + 1), ex), -1: (x * 4 + wrap(z - 1), ex)}
    dev_y = {1: (dp, wrap(y + 1) * 2 + c), -1: (dp, wrap(y - 1) * 2 + c)}
    dev_c = (dp, y * 2 + oc)

    counter = [0]
    sent = []

    def fresh(n=1):
        first = counter[0]
        counter[0] += n
        assert counter[0] <= N_COPIES
        return first

    def copy(i, src, dst, dev):
        return pltpu.make_async_remote_copy(
            src_ref=src, dst_ref=dst, send_sem=send_sem.at[i], recv_sem=recv_sem.at[i],
            device_id=dev, device_id_type=MESH,
        )

    def send(i, src, dst, dev):
        d = copy(i, src, dst, dev)
        d.start()
        sent.append(d)

    def recv(i, landing, dev):
        copy(i, landing, landing, dev).wait_recv()

    locals_open = []

    def local(src, dst):
        d = pltpu.make_async_copy(src, dst, local_sem.at[len(locals_open)])
        d.start()
        locals_open.append(d)
        return d

    load_tok = local(tok_hbm, tok)
    load_cot = local(cot_hbm, cot)
    load_wi = local(wi_hbm, wi)
    load_wo = local(wo_hbm, wo)

    barrier = pltpu.get_barrier_semaphore()
    for dev in (dev_x[1], dev_x[-1], dev_z[1], dev_z[-1], dev_y[1], dev_y[-1], dev_c):
        pl.semaphore_signal(barrier, inc=1, device_id=dev, device_id_type=MESH)

    def pick(t):
        if t == 0:
            load_tok.wait()
            got = dot(pick_ref[...], tok[...]).astype(BF)
        else:
            load_cot.wait()
            got = (gate_ref[:, 0:1] * dot(pick_ref[...], cot[...])).astype(BF)
        for ph in range(2):
            for h in range(2):
                ag[t, ph, h, x, z] = got[32 * ph:32 * ph + 32, 512 * h:512 * h + 512]

    class Gather:
        def __init__(self, buf, h, lead):
            self.buf, self.h, self.lead = buf, h, lead
            self.f, self.s = (x, z) if h == 0 else (z, x)
            self.fd, self.sd = (dev_x, dev_z) if h == 0 else (dev_z, dev_x)
            self.i = fresh(8)

        def blk(self, fi, si):
            where = (fi, si) if self.h == 0 else (si, fi)
            return self.buf.at[self.lead + where]

        def grp(self, si, first, n):
            where = (pl.ds(first, n), si) if self.h == 0 else (si, pl.ds(first, n))
            return self.buf.at[self.lead + where]

        def s1(self):
            b = self.blk(self.f, self.s)
            send(self.i, b, b, self.fd[1])
            send(self.i + 1, b, b, self.fd[-1])

        def s2(self):
            for n, d in ((0, 1), (1, -1)):
                b = self.blk(wrap(self.f - d), self.s)
                recv(self.i + n, b, self.fd[d])
                b = b.at[pl.ds(16 * n, 16)]
                send(self.i + 2 + n, b, b, self.fd[d])

        def s4(self):
            for n, d in ((0, 1), (1, -1)):
                b = self.blk(wrap(self.f + 2), self.s).at[pl.ds(16 * n, 16)]
                recv(self.i + 2 + n, b, self.fd[d])
            g = self.grp(self.s, 0, 4)
            send(self.i + 4, g, g, self.sd[1])
            send(self.i + 5, g, g, self.sd[-1])

        def s5(self):
            for n, d in ((0, 1), (1, -1)):
                recv(self.i + 4 + n, self.grp(wrap(self.s - d), 0, 4), self.sd[d])
                g = self.grp(wrap(self.s - d), 2 * n, 2)
                send(self.i + 6 + n, g, g, self.sd[d])

        def s6(self):
            for n, d in ((0, 1), (1, -1)):
                recv(self.i + 6 + n, self.grp(wrap(self.s + 2), 2 * n, 2), self.sd[d])

    class Counts:
        def __init__(self):
            self.i = fresh(6)

        def s1(self):
            b = cnt.at[x, z]
            send(self.i, b, b, dev_x[1])
            send(self.i + 1, b, b, dev_x[-1])

        def s2(self):
            recv(self.i, cnt.at[wrap(x - 1), z], dev_x[1])
            recv(self.i + 1, cnt.at[wrap(x + 1), z], dev_x[-1])
            b = cnt.at[wrap(x - 1), z]
            send(self.i + 2, b, b, dev_x[1])

        def s4(self):
            recv(self.i + 2, cnt.at[wrap(x + 2), z], dev_x[1])
            b = cnt.at[:, z]
            send(self.i + 3, b, b, dev_z[1])
            send(self.i + 4, b, b, dev_z[-1])

        def s5(self):
            recv(self.i + 3, cnt.at[:, wrap(z - 1)], dev_z[1])
            recv(self.i + 4, cnt.at[:, wrap(z + 1)], dev_z[-1])
            b = cnt.at[:, wrap(z - 1)]
            send(self.i + 5, b, b, dev_z[1])

        def s6(self):
            recv(self.i + 5, cnt.at[:, wrap(z + 2)], dev_z[1])

    class Both:
        def __init__(self, t, ph):
            self.parts = [Gather(ag, h, (t, ph, h)) for h in range(2)]

        def __getattr__(self, name):
            return lambda: [getattr(p, name)() for p in self.parts]

    def places():
        first, second = [], []
        total = jnp.zeros((8, 128), jnp.int32)
        for i in range(16):
            held = jnp.minimum(cnt[i // 4, i % 4], 32)
            first.append((total, held))
            total = total + held
        for i in range(16):
            held = jnp.maximum(cnt[i // 4, i % 4] - 32, 0)
            second.append((total, held))
            total = total + held
        return first, second

    def lane_places(shards):
        lane = lax.broadcasted_iota(jnp.int32, (8, 128), 1)
        quarter, slot = lane // 32, lane % 32
        tiles = []
        for b in range(4):
            start, held = shards[4 * b + 3]
            for j in (2, 1, 0):
                start = jnp.where(quarter == j, shards[4 * b + j][0], start)
                held = jnp.where(quarter == j, shards[4 * b + j][1], held)
            tiles.append(jnp.where(slot < held, start + slot, -1))
        return tiles

    def build_c():
        first, second = places()
        row = lax.broadcasted_iota(jnp.int32, (256, 128), 0)
        for n, (shards, k) in enumerate(((first, 0), (first, 1), (second, 1))):
            for b, tile in enumerate(lane_places(shards)):
                hit = jnp.broadcast_to(tile[0:1], (256, 128)) == row + 256 * k
                c_mat[n, :, 128 * b:128 * b + 128] = jnp.where(hit, 1.0, 0.0).astype(BF)

    def build_ct():
        first, second = places()
        slot = lax.broadcasted_iota(jnp.int32, (32, 128), 0)
        lane = lax.broadcasted_iota(jnp.int32, (32, 128), 1)
        for i in range(16):
            for ph, shards in ((0, first), (1, second)):
                start = jnp.broadcast_to(shards[i][0][0:1], (32, 128))
                held = jnp.broadcast_to(shards[i][1][0:1], (32, 128))
                place = jnp.where(slot < held, start + slot, -1)
                for b in range(4):
                    hit = place == lane + 128 * b
                    ct[i // 4, i % 4, 32 * ph:32 * ph + 32, 128 * b:128 * b + 128] = jnp.where(
                        hit, 1.0, 0.0
                    ).astype(BF)

    def compact(t, k):
        for h in range(2):
            if k == 0:
                got = dot(c_mat[0], ag[t, 0, h].reshape(512, 512))
            else:
                got = dot(c_mat[1], ag[t, 0, h].reshape(512, 512))
                got += dot(c_mat[2], ag[t, 1, h].reshape(512, 512))
            rows[t, 256 * k:256 * k + 256, 512 * h:512 * h + 512] = got.astype(BF)

    def hidden_cols(core, yy):
        return pl.ds(pl.multiple_of(core * 1024 + yy * 256, 256), 256)

    class Reduce:
        def __init__(self, t, k):
            self.t, self.k = t, k
            self.ic, self.io, self.inb = fresh(4), fresh(2), fresh(2)

        def tile(self, core, yy):
            left = rows[self.t, 256 * self.k:256 * self.k + 256, :]
            if self.t == 0:
                return dot(left, wi[:, hidden_cols(core, yy)])
            return dot(left, wo[hidden_cols(core, yy), :], NT)

        def m1(self):
            t, k = self.t, self.k

            def step(j, carry):
                yy = wrap(y + 2 - j)
                xs[t, k, yy] = self.tile(oc, yy).astype(BF)
                copy(self.ic + yy, xs.at[t, k, yy], xr.at[t, k, yy], dev_c).start()
                return carry

            lax.fori_loop(0, 4, step, 0)

        def own_tile(self, yy):
            t, k = self.t, self.k
            got = self.tile(c, yy)
            copy(self.ic + yy, xs.at[t, k, yy], xr.at[t, k, yy], dev_c).wait_recv()
            return got + xr[t, k, yy].astype(F32)

        def m2(self):
            t, k = self.t, self.k
            ps[t, k, 0] = self.own_tile(wrap(y + 2)).astype(BF)
            for n, d in ((0, 1), (1, -1)):
                send(
                    self.io + n, ps.at[t, k, 0, pl.ds(128 * n, 128)], opp_rx.at[t, k, n], dev_y[d]
                )

            def step(j, carry):
                acc[t, k, j - 1] = self.own_tile(wrap(y + 2 - j))
                return carry

            lax.fori_loop(1, 4, step, 0)

        def nbr(self):
            t, k = self.t, self.k
            for n, d in ((0, 1), (1, -1)):
                recv(self.io + n, opp_rx.at[t, k, n], dev_y[d])
                here = pl.ds(128 * n, 128)
                away = pl.ds(128 * (1 - n), 128)
                j = 0 if d == 1 else 2
                ps[t, k, 1 + n, here] = (
                    acc[t, k, j, here] + opp_rx[t, k, n].astype(F32)
                ).astype(BF)
                ps[t, k, 1 + n, away] = acc[t, k, j, away].astype(BF)
                send(self.inb + n, ps.at[t, k, 1 + n], nbr_rx.at[t, k, n], dev_y[d])

        def total(self):
            t, k = self.t, self.k
            for n, d in ((0, 1), (1, -1)):
                recv(self.inb + n, nbr_rx.at[t, k, n], dev_y[d])
            return acc[t, k, 1] + nbr_rx[t, k, 0].astype(F32) + nbr_rx[t, k, 1].astype(F32)

        def wait_sent(self):
            t, k = self.t, self.k

            def step(yy, carry):
                copy(self.ic + yy, xs.at[t, k, yy], xr.at[t, k, yy], dev_c).wait_send()
                return carry

            lax.fori_loop(0, 4, step, 0)

    class Share:
        def __init__(self, t, k):
            self.t, self.k = t, k
            self.iy, self.io, self.ic = fresh(2), fresh(2), fresh(4)

        def piece(self, core, yy):
            return hb.at[self.t, pl.ds(256 * self.k, 256), hidden_cols(core, yy)]

        def half(self, core, yy, n):
            return hb.at[self.t, pl.ds(256 * self.k + 128 * n, 128), hidden_cols(core, yy)]

        def own(self, value):
            hb[self.t, pl.ds(256 * self.k, 256), hidden_cols(c, y)] = value.astype(BF)
            p = self.piece(c, y)
            send(self.iy, p, p, dev_y[1])
            send(self.iy + 1, p, p, dev_y[-1])
            send(self.ic, p, p, dev_c)

        def fwd(self):
            for n, d in ((0, 1), (1, -1)):
                p = self.piece(c, wrap(y - d))
                recv(self.iy + n, p, dev_y[d])
                q = self.half(c, wrap(y - d), n)
                send(self.io + n, q, q, dev_y[d])
                send(self.ic + 1 + n, p, p, dev_c)

        def opp(self):
            for n, d in ((0, 1), (1, -1)):
                recv(self.io + n, self.half(c, wrap(y + 2), n), dev_y[d])
            p = self.piece(c, wrap(y + 2))
            send(self.ic + 3, p, p, dev_c)

        def done(self):
            for n, yy in enumerate((y, wrap(y - 1), wrap(y + 1), wrap(y + 2))):
                recv(self.ic + n, self.piece(oc, yy), dev_c)

    def contract(t, k):
        def step(n, carry):
            cols = pl.ds(pl.multiple_of(n * 256, 256), 256)
            left = hb[t, 256 * k:256 * k + 256, :]
            got = dot(left, wo[:, cols]) if t == 0 else dot(left, wi[cols, :], NT)
            part[t, 256 * k:256 * k + 256, cols] = got.astype(BF)
            return carry

        lax.fori_loop(0, 4, step, 0)

    class Home:
        def __init__(self, t, h):
            self.t, self.h = t, h
            self.f, self.s = (x, z) if h == 0 else (z, x)
            self.fd, self.sd = (dev_x, dev_z) if h == 0 else (dev_z, dev_x)
            self.i = fresh(8)

        def group(self, fi):
            picks = ct[fi] if self.h == 0 else ct[:, fi]
            got = dot(picks.reshape(256, 512), part[self.t, :, 512 * self.h:512 * self.h + 512])
            return got.reshape(4, 64, 512)

        def f1(self):
            t, h = self.t, self.h
            spread[t, h, 0] = self.group(wrap(self.f + 2)).astype(BF)
            for n, d in ((0, 1), (1, -1)):
                send(
                    self.i + n, spread.at[t, h, 0, pl.ds(2 * n, 2)], f_opp.at[t, h, n], self.fd[d]
                )

        def f2(self):
            t, h = self.t, self.h
            for n, d in ((0, 1), (1, -1)):
                got = self.group(wrap(self.f + d))
                recv(self.i + n, f_opp.at[t, h, n], self.fd[d])
                near = got[2 * n:2 * n + 2] + f_opp[t, h, n].astype(F32)
                spread[t, h, 1 + n, 2 * n:2 * n + 2] = near.astype(BF)
                spread[t, h, 1 + n, 2 - 2 * n:4 - 2 * n] = got[2 - 2 * n:4 - 2 * n].astype(BF)
                send(self.i + 2 + n, spread.at[t, h, 1 + n], f_nbr.at[t, h, n], self.fd[d])

        def f3(self):
            t, h = self.t, self.h
            got = self.group(self.f)
            for n, d in ((0, 1), (1, -1)):
                recv(self.i + 2 + n, f_nbr.at[t, h, n], self.fd[d])
            got = got + f_nbr[t, h, 0].astype(F32) + f_nbr[t, h, 1].astype(F32)
            grouped[t, h] = got.astype(BF)
            far = wrap(self.s + 2)
            for n, d in ((0, 1), (1, -1)):
                send(
                    self.i + 4 + n, grouped.at[t, h, far, pl.ds(32 * n, 32)], s_opp.at[t, h, n],
                    self.sd[d],
                )

        def g2(self):
            t, h = self.t, self.h
            for n, d in ((0, 1), (1, -1)):
                recv(self.i + 4 + n, s_opp.at[t, h, n], self.sd[d])
                to = wrap(self.s + d)
                here = pl.ds(32 * n, 32)
                grouped[t, h, to, here] = (
                    grouped[t, h, to, here].astype(F32) + s_opp[t, h, n].astype(F32)
                ).astype(BF)
                send(self.i + 6 + n, grouped.at[t, h, to], s_nbr.at[t, h, n], self.sd[d])

        def g3(self):
            t, h = self.t, self.h
            for n, d in ((0, 1), (1, -1)):
                recv(self.i + 6 + n, s_nbr.at[t, h, n], self.sd[d])
            got = (
                grouped[t, h, self.s].astype(F32)
                + s_nbr[t, h, 0].astype(F32)
                + s_nbr[t, h, 1].astype(F32)
            )
            if t == 0:
                got = gate_ref[:, 0:1] * got
            slots_out[t, :, 512 * h:512 * h + 512] = got.astype(BF)

    class HomeBoth:
        def __init__(self, t):
            self.parts = [Home(t, h) for h in range(2)]

        def __getattr__(self, name):
            return lambda: [getattr(p, name)() for p in self.parts]

    r_a, r_b, g_a, g_b = Both(0, 0), Both(0, 1), Both(1, 0), Both(1, 1)
    meta = Counts()
    pre = [Reduce(0, 0), Reduce(0, 1)]
    back = [Reduce(1, 0), Reduce(1, 1)]
    hid = [Share(0, 0), Share(0, 1)]
    bpre = [Share(1, 0), Share(1, 1)]
    mixed, d_tok = HomeBoth(0), HomeBoth(1)

    def fin_pre(k):
        activated, slopes = gelu_pair(pre[k].total())
        slope[k] = slopes
        hid[k].own(activated)

    def fin_back(k):
        bpre[k].own(back[k].total() * slope[k])

    cnt[x, z] = count_ref[...]
    pick(0)
    pl.semaphore_wait(barrier, 7)
    r_a.s1()
    meta.s1()
    r_b.s1()
    pick(1)
    r_a.s2()
    meta.s2()
    r_a.s4()
    meta.s4()
    r_b.s2()
    r_a.s5()
    meta.s5()
    r_b.s4()
    meta.s6()
    build_c()
    g_a.s1()
    g_b.s1()
    r_a.s6()
    compact(0, 0)
    load_wi.wait()
    pre[0].m1()
    pre[0].m2()
    r_b.s5()
    g_a.s2()
    g_b.s2()
    g_a.s4()
    pre[0].nbr()
    r_b.s6()
    compact(0, 1)
    pre[1].m1()
    pre[1].m2()
    out_rows = local(rows.at[0], rows_out.at[0])
    g_a.s5()
    g_b.s4()
    fin_pre(0)
    pre[1].nbr()
    g_a.s6()
    compact(1, 0)
    load_wo.wait()
    back[0].m1()
    back[0].m2()
    g_b.s5()
    hid[0].fwd()
    fin_pre(1)
    back[0].nbr()
    g_b.s6()
    compact(1, 1)
    back[1].m1()
    back[1].m2()
    out_grads = local(rows.at[1], rows_out.at[1])
    hid[0].opp()
    hid[1].fwd()
    fin_back(0)
    back[1].nbr()
    build_ct()
    hid[0].done()
    contract(0, 0)
    hid[1].opp()
    bpre[0].fwd()
    hid[1].done()
    out_hid = local(hb.at[0], hb_out.at[0])
    fin_back(1)
    contract(0, 1)
    mixed.f1()
    bpre[0].opp()
    mixed.f2()
    bpre[1].fwd()
    bpre[0].done()
    contract(1, 0)
    mixed.f3()
    bpre[1].opp()
    mixed.g2()
    bpre[1].done()
    out_bp = local(hb.at[1], hb_out.at[1])
    contract(1, 1)
    d_tok.f1()
    mixed.g3()
    d_tok.f2()
    d_tok.f3()
    d_tok.g2()
    d_tok.g3()

    for r in pre + back:
        r.wait_sent()
    for d in sent:
        d.wait_send()
    for d in (out_rows, out_grads, out_hid, out_bp):
        d.wait()


def exchange(pick, gate, count, tokens, cotangent, w_in, w_out):
    vmem = pl.BlockSpec(memory_space=pltpu.VMEM)
    anywhere = pl.BlockSpec(memory_space=pl.ANY)

    def v(*shape, dtype=BF):
        return pltpu.VMEM(shape, dtype)

    return pl.pallas_call(
        kernel,
        out_shape=(
            jax.ShapeDtypeStruct((2, 512, 1024), BF),
            jax.ShapeDtypeStruct((2, 512, 2048), BF),
            jax.ShapeDtypeStruct((2, 64, 1024), BF),
        ),
        in_specs=[vmem] * 3 + [anywhere] * 4,
        out_specs=(anywhere, anywhere, vmem),
        scratch_shapes=[
            v(256, 1024), v(256, 1024), v(1024, 2048), v(2048, 1024),
            v(2, 2, 2, 4, 4, 32, 512),
            v(4, 4, 8, 128, dtype=jnp.int32),
            v(3, 256, 512),
            v(4, 4, 64, 512),
            v(2, 512, 1024),
            v(2, 2, 4, 256, 256), v(2, 2, 4, 256, 256),
            v(2, 2, 3, 256, 256),
            v(2, 2, 2, 128, 256),
            v(2, 2, 2, 256, 256),
            v(2, 2, 3, 256, 256, dtype=F32),
            v(2, 256, 256, dtype=F32),
            v(2, 512, 2048),
            v(2, 512, 1024),
            v(2, 2, 3, 4, 64, 512),
            v(2, 2, 2, 2, 64, 512),
            v(2, 2, 2, 4, 64, 512),
            v(2, 2, 4, 64, 512),
            v(2, 2, 2, 32, 512),
            v(2, 2, 2, 64, 512),
            pltpu.SemaphoreType.DMA((N_COPIES,)),
            pltpu.SemaphoreType.DMA((N_COPIES,)),
            pltpu.SemaphoreType.DMA((N_LOCAL,)),
        ],
        compiler_params=pltpu.CompilerParams(
            collective_id=0, has_side_effects=True, vmem_limit_bytes=60 * 2**20
        ),
        cost_estimate=pl.CostEstimate(
            flops=10 * 10**9, bytes_accessed=20 * 2**20, transcendentals=2**19
        ),
    )(pick, gate, count, tokens, cotangent, w_in, w_out)


def local(tokens, w_in, w_out, chosen, counts, gates, cotangent):
    places = chosen[0]
    live = jnp.arange(64) < counts[0]
    spots = jnp.arange(256)
    pick = ((places[:, None] == spots[None, :]) & live[:, None]).astype(BF)
    gate = jnp.broadcast_to(gates[0][:, None], (64, 128))
    count = jnp.broadcast_to(counts[0], (8, 128))
    rows, hb, slots = exchange(pick, gate, count, tokens, cotangent, w_in, w_out)

    def tall(a, b):
        return lax.dot_general(
            a, b, (((0,), (0,)), ((), ())), preferred_element_type=F32
        ).astype(BF)

    return (
        tall(pick, slots[0]),
        tall(pick, slots[1]),
        tall(rows[0], hb[1]),
        tall(hb[0], rows[1]),
    )


def solution(mesh):
    in_specs = (
        P("dp", "expert"),
        P("expert", "dp"),
        P("dp", "expert"),
        P("dp", None),
        P("dp"),
        P("dp", None),
        P("dp", "expert"),
    )
    out_specs = (P("dp", "expert"), P("dp", "expert"), P("expert", "dp"), P("dp", "expert"))
    return jax.shard_map(local, mesh=mesh, in_specs=in_specs, out_specs=out_specs, check_vma=False)
```

```python
import jax
import jax.numpy as jnp
from jax import lax
from jax.experimental import pallas as pl
from jax.experimental.pallas import tpu as pltpu
from jax.sharding import PartitionSpec as P

half_root = 0.7071067811865476
inv_root_tau = 0.3989422804014327

MESH = pl.DeviceIdType.MESH
BF = jnp.bfloat16
F32 = jnp.float32

N_COPIES = 200
N_LOCAL = 24

ORDER = (
    "pick0", "ag1_00", "ag1_01", "pick1", "ag1_10", "meta1", "ag2_00", "ag2_01", "meta2",
    "ag3_00", "ag3_01", "ag1_11", "ag2_10", "meta", "buildc", "ag4_00", "cmp_00", "ma_00",
    "ag4_01", "mb_00", "cmp_01", "ma_01", "mc_00", "mb_01", "md_00", "nb_00", "ag3_10", "mc_01",
    "buildct", "ag2_11", "md_01", "nb_01", "fin_00", "ag3_11", "fin_01", "ag4_10", "cmp_10",
    "ma_10", "ag4_11", "cmp_11", "fwd_00", "ma_11", "mb_10", "mc_10", "mb_11", "mc_11", "fwd_01",
    "opp_00", "md_11", "md_10", "nb_10", "ct_00", "opp_01", "nb_11", "ct_01", "fin_10", "e0_0",
    "e1_0", "fin_11", "dwo0", "fn0_0", "fn1_0", "fwd_10", "e2_0", "dwo1", "fn2_0", "dwo2",
    "fn3_0", "fs0_0", "fwd_11", "fs1_0", "opp_10", "ct1_11", "fs2_0", "opp_11", "ct_10", "ct2_11",
    "e0_1", "e1_1", "fs3_0", "dwi0", "dwo3", "fn0_1", "dwo4", "fn1_1", "g3_0", "fn2_1", "dwo5",
    "dwo6", "fn3_1", "dwi1", "dwi2", "e2_1", "fs0_1", "fs1_1", "fs2_1", "fs3_1", "dwo7", "dwi3",
    "g3_1",
)

NN = (((1,), (0,)), ((), ()))
NT = (((1,), (1,)), ((), ()))
TN = (((0,), (0,)), ((), ()))


def dot(a, b, dims=NN):
    return lax.dot_general(a, b, dims, preferred_element_type=F32)


def gelu_pair(pre_act):
    cdf_part = 0.5 * (1.0 + lax.erf(pre_act * half_root))
    slopes = cdf_part + pre_act * jnp.exp(-0.5 * pre_act * pre_act) * inv_root_tau
    return (pre_act * cdf_part, slopes)


def wrap(v):
    return lax.rem(v + 8, 4)


def kernel(
    chosen_ref, gates_ref, count_ref, tok_hbm, cot_hbm, wi_hbm, wo_hbm,
    pick_out, slots_out, dwi_out, dwo_out,
    tok, cot, wi, wo, gate, ag, cnt, c_mat, ct, rows, xs, xr, ps, opp_rx, nbr_rx, acc, slope, hb,
    sub, part, spread, home, f_opp, f_nbr, grouped, s_rx, dwi, dwo,
    send_sem, recv_sem, local_sem,
):
    dp, ex = lax.axis_index("dp"), lax.axis_index("expert")
    x, z = lax.div(dp, 4), lax.rem(dp, 4)
    y, c = lax.div(ex, 2), lax.rem(ex, 2)
    oc = 1 - c
    dev_x = {d: (wrap(x + d) * 4 + z, ex) for d in (1, -1, 2)}
    dev_z = {d: (x * 4 + wrap(z + d), ex) for d in (1, -1, 2)}
    dev_y = {d: (dp, wrap(y + d) * 2 + c) for d in (1, -1)}
    dev_c = (dp, y * 2 + oc)
    both = ((0, 1), (1, -1))
    three = ((0, 1), (1, -1), (2, 2))

    counter = [0]
    sent = []

    def fresh(n):
        first = counter[0]
        counter[0] += n
        assert counter[0] <= N_COPIES
        return first

    def copy(i, src, dst, dev):
        return pltpu.make_async_remote_copy(
            src_ref=src, dst_ref=dst, send_sem=send_sem.at[i], recv_sem=recv_sem.at[i],
            device_id=dev, device_id_type=MESH,
        )

    def send(i, src, dst, dev):
        d = copy(i, src, dst, dev)
        d.start()
        sent.append(d)

    def recv(i, landing, dev):
        copy(i, landing, landing, dev).wait_recv()

    opened = []

    def local_copy(src, dst):
        d = pltpu.make_async_copy(src, dst, local_sem.at[len(opened)])
        d.start()
        opened.append(d)
        return d

    load = {
        "tok": local_copy(tok_hbm, tok),
        "cot": local_copy(cot_hbm, cot),
        0: local_copy(wi_hbm, wi),
        1: local_copy(wo_hbm, wo),
    }

    barrier = pltpu.get_barrier_semaphore()
    partners = [dev_x[d] for d in dev_x] + [dev_z[d] for d in dev_z] + [dev_y[1], dev_y[-1], dev_c]
    for dev in partners:
        pl.semaphore_signal(barrier, inc=1, device_id=dev, device_id_type=MESH)

    tasks = {}

    def column(row):
        here = lax.broadcasted_iota(jnp.int32, (64, 64), 0)
        there = lax.broadcasted_iota(jnp.int32, (64, 64), 1)
        wide = jnp.broadcast_to(row.astype(F32), (64, 64))
        return jnp.sum(jnp.where(here == there, wide, 0.0), axis=1, keepdims=True)

    def pick0():
        place = jnp.broadcast_to(column(chosen_ref[...]), (64, 256)).astype(jnp.int32)
        spot = lax.broadcasted_iota(jnp.int32, (64, 256), 1)
        slot = lax.broadcasted_iota(jnp.int32, (64, 256), 0)
        held = jnp.broadcast_to(count_ref[0], (64, 256))
        hit = jnp.where(place == spot, 1.0, 0.0) * jnp.where(slot < held, 1.0, 0.0)
        pick_out[...] = hit.astype(BF)
        gate[...] = jnp.broadcast_to(column(gates_ref[...]), (64, 128))
        cnt[x, z] = jnp.broadcast_to(count_ref[0], (8, 128))
        load["tok"].wait()
        keep(0, dot(pick_out[...], tok[...]).astype(BF))

    def pick1():
        load["cot"].wait()
        keep(1, (gate[:, 0:1] * dot(pick_out[...], cot[...])).astype(BF))

    def keep(t, got):
        for ph in range(2):
            for h in range(2):
                ag[t, ph, h, x, z] = got[32 * ph:32 * ph + 32, 512 * h:512 * h + 512]

    tasks["pick0"], tasks["pick1"] = pick0, pick1

    def axes(h):
        return (x, z, dev_x, dev_z) if h == 0 else (z, x, dev_z, dev_x)

    def add_gather(t, ph):
        base = [fresh(7), fresh(7)]

        def blk(h, fi, si):
            return ag.at[(t, ph, h) + ((fi, si) if h == 0 else (si, fi))]

        def grp(h, si, first, n):
            many = pl.ds(first, n)
            return ag.at[(t, ph, h) + ((many, si) if h == 0 else (si, many))]

        def ag1():
            for h in range(2):
                f, s, fd, sd = axes(h)
                for n, d in three:
                    send(base[h] + n, blk(h, f, s), blk(h, f, s), fd[d])

        def ag2():
            for h in range(2):
                f, s, fd, sd = axes(h)
                for n, d in three:
                    recv(base[h] + n, blk(h, wrap(f - d), s), fd[d])
                for n, d in both:
                    send(base[h] + 3 + n, grp(h, s, 0, 4), grp(h, s, 0, 4), sd[d])

        def ag3():
            for h in range(2):
                f, s, fd, sd = axes(h)
                for n, d in both:
                    recv(base[h] + 3 + n, grp(h, wrap(s - d), 0, 4), sd[d])
                    g = grp(h, wrap(s - d), 2 * n, 2)
                    send(base[h] + 5 + n, g, g, sd[d])

        def ag4():
            for h in range(2):
                f, s, fd, sd = axes(h)
                for n, d in both:
                    recv(base[h] + 5 + n, grp(h, wrap(s + 2), 2 * n, 2), sd[d])

        for name, f in (("ag1", ag1), ("ag2", ag2), ("ag3", ag3), ("ag4", ag4)):
            tasks[f"{name}_{t}{ph}"] = f

    meta_base = fresh(6)

    def meta1():
        for n, d in three:
            send(meta_base + n, cnt.at[x, z], cnt.at[x, z], dev_x[d])

    def meta2():
        for n, d in three:
            recv(meta_base + n, cnt.at[wrap(x - d), z], dev_x[d])
        for n, d in three:
            send(meta_base + 3 + n, cnt.at[:, z], cnt.at[:, z], dev_z[d])

    def meta():
        for n, d in three:
            recv(meta_base + 3 + n, cnt.at[:, wrap(z - d)], dev_z[d])

    tasks.update(meta1=meta1, meta2=meta2, meta=meta)

    def places():
        first, second = [], []
        total = jnp.zeros((8, 128), jnp.int32)
        for i in range(16):
            held = jnp.minimum(cnt[i // 4, i % 4], 32)
            first.append((total, held))
            total = total + held
        for i in range(16):
            held = jnp.maximum(cnt[i // 4, i % 4] - 32, 0)
            second.append((total, held))
            total = total + held
        return first, second

    def lane_places(shards):
        lane = lax.broadcasted_iota(jnp.int32, (8, 128), 1)
        quarter, slot = lane // 32, lane % 32
        tiles = []
        for b in range(4):
            start, held = shards[4 * b + 3]
            for j in (2, 1, 0):
                start = jnp.where(quarter == j, shards[4 * b + j][0], start)
                held = jnp.where(quarter == j, shards[4 * b + j][1], held)
            tiles.append(jnp.where(slot < held, start + slot, -1))
        return tiles

    def buildc():
        first, second = places()
        row = lax.broadcasted_iota(jnp.int32, (256, 128), 0)
        for n, (shards, k) in enumerate(((first, 0), (first, 1), (second, 1))):
            for b, tile in enumerate(lane_places(shards)):
                hit = jnp.broadcast_to(tile[0:1], (256, 128)) == row + 256 * k
                c_mat[n, :, 128 * b:128 * b + 128] = jnp.where(hit, 1.0, 0.0).astype(BF)

    def buildct():
        first, second = places()
        slot = lax.broadcasted_iota(jnp.int32, (32, 128), 0)
        lane = lax.broadcasted_iota(jnp.int32, (32, 128), 1)
        for i in range(16):
            for ph, shards in ((0, first), (1, second)):
                start = jnp.broadcast_to(shards[i][0][0:1], (32, 128))
                held = jnp.broadcast_to(shards[i][1][0:1], (32, 128))
                place = jnp.where(slot < held, start + slot, -1)
                for b in range(4):
                    hit = place == lane + 128 * b
                    ct[i // 4, i % 4, 32 * ph:32 * ph + 32, 128 * b:128 * b + 128] = jnp.where(
                        hit, 1.0, 0.0
                    ).astype(BF)

    tasks["buildc"], tasks["buildct"] = buildc, buildct

    def hidden_cols(core, yy, width=256):
        return pl.ds(pl.multiple_of(core * 1024 + yy * width, width), width)

    def add_chunk(t, k):
        mine = pl.ds(256 * k, 256)
        ic, io, inb = fresh(2), fresh(2), fresh(2)
        iy, iw, ih = fresh(2), fresh(2), fresh(4)
        far = lax.div(wrap(y + 2), 2)
        near = 1 - far

        def cmp():
            for h in range(2):
                cols = slice(512 * h, 512 * h + 512)
                got = dot(c_mat[k], ag[t, 0, h].reshape(512, 512))
                if k == 1:
                    got += dot(c_mat[2], ag[t, 1, h].reshape(512, 512))
                rows[t, mine, cols] = got.astype(BF)

        def pair(core, p):
            left = rows[t, mine, :]
            if t == 0:
                return dot(left, wi[:, hidden_cols(core, p, 512)])
            return dot(left, wo[hidden_cols(core, p, 512), :], NT)

        def for_other(p, n):
            got = pair(oc, p).astype(BF)
            xs[t, k, p, 0] = got[:, :256]
            xs[t, k, p, 1] = got[:, 256:]
            send(ic + n, xs.at[t, k, p], xr.at[t, k, p], dev_c)

        def for_self(p, n):
            got = pair(c, p)
            recv(ic + n, xr.at[t, k, p], dev_c)
            acc[t, k, p, 0] = got[:, :256] + xr[t, k, p, 0].astype(F32)
            acc[t, k, p, 1] = got[:, 256:] + xr[t, k, p, 1].astype(F32)

        def tile(yy):
            return (t, k, lax.div(yy, 2), lax.rem(yy, 2))

        def ma():
            if k == 0:
                load[t].wait()
            for_other(far, 0)

        def mb():
            for_self(far, 0)
            ps[t, k, 0] = acc[tile(wrap(y + 2))].astype(BF)
            for n, d in both:
                send(io + n, ps.at[t, k, 0, pl.ds(128 * n, 128)], opp_rx.at[t, k, n], dev_y[d])

        def mc():
            for_other(near, 1)

        def md():
            for_self(near, 1)

        def nb():
            for n, d in both:
                recv(io + n, opp_rx.at[t, k, n], dev_y[d])
                got = acc[tile(wrap(y + d))]
                here = slice(128 * n, 128 * n + 128)
                away = slice(128 - 128 * n, 256 - 128 * n)
                ps[t, k, 1 + n, here] = (got[here] + opp_rx[t, k, n].astype(F32)).astype(BF)
                ps[t, k, 1 + n, away] = got[away].astype(BF)
                send(inb + n, ps.at[t, k, 1 + n], nbr_rx.at[t, k, n], dev_y[d])

        def piece(core, yy):
            return hb.at[t, mine, hidden_cols(core, yy)]

        def half(yy, n):
            return hb.at[t, pl.ds(256 * k + 128 * n, 128), hidden_cols(c, yy)]

        def fin():
            for n, d in both:
                recv(inb + n, nbr_rx.at[t, k, n], dev_y[d])
            total = acc[tile(y)] + nbr_rx[t, k, 0].astype(F32) + nbr_rx[t, k, 1].astype(F32)
            if t == 0:
                total, slopes = gelu_pair(total)
                slope[k] = slopes
            else:
                total = total * slope[k]
            hb[t, mine, hidden_cols(c, y)] = total.astype(BF)
            p = piece(c, y)
            send(iy, p, p, dev_y[1])
            send(iy + 1, p, p, dev_y[-1])
            send(ih, p, p, dev_c)

        def fwd():
            for n, d in both:
                p, q = piece(c, wrap(y - d)), half(wrap(y - d), n)
                recv(iy + n, p, dev_y[d])
                send(iw + n, q, q, dev_y[d])
                send(ih + 1 + n, p, p, dev_c)

        def opp():
            for n, d in both:
                recv(iw + n, half(wrap(y + 2), n), dev_y[d])
            p = piece(c, wrap(y + 2))
            send(ih + 3, p, p, dev_c)

        def near_in():
            for n, yy in enumerate((y, wrap(y - 1), wrap(y + 1))):
                recv(ih + n, piece(oc, yy), dev_c)

        def far_in():
            recv(ih + 3, piece(oc, wrap(y + 2)), dev_c)

        def whole():
            near_in()
            far_in()

            def step(n, carry):
                cols = pl.ds(pl.multiple_of(n * 256, 256), 256)
                left = hb[t, mine, :]
                got = dot(left, wo[:, cols]) if t == 0 else dot(left, wi[cols, :], NT)
                part[t, mine, cols] = got.astype(BF)
                return carry

            lax.fori_loop(0, 4, step, 0)

        def product(core, yy):
            units = hidden_cols(core, yy)
            left = hb[t, mine, units]
            return dot(left, wo[units, :]) if t == 0 else dot(left, wi[:, units], NT)

        def ct1():
            near_in()
            sub[...] = product(c, y)

            def step(n, carry):
                sub[...] += product(lax.rem(c + lax.div(n, 3), 2), wrap(y + 3 + lax.rem(n, 3)))
                return carry

            lax.fori_loop(0, 1, lambda n, carry: step(2, carry), 0)
            lax.fori_loop(3, 6, step, 0)
            lax.fori_loop(0, 1, step, 0)

        def ct2():
            far_in()
            got = sub[...] + product(c, wrap(y + 2)) + product(oc, wrap(y + 2))
            part[t, mine, :] = got.astype(BF)

        for f in (cmp, ma, mb, mc, md, nb, fin, fwd, opp):
            tasks[f"{f.__name__}_{t}{k}"] = f
        if (t, k) == (1, 1):
            tasks["ct1_11"], tasks["ct2_11"] = ct1, ct2
        else:
            tasks[f"ct_{t}{k}"] = whole

    def add_home(t):
        base = [fresh(19), fresh(19)]

        def group(h, fi):
            picks = ct[fi] if h == 0 else ct[:, fi]
            got = dot(picks.reshape(256, 512), part[t, :, 512 * h:512 * h + 512])
            return got.reshape(4, 64, 512)

        def e0():
            for h in range(2):
                f, s, fd, sd = axes(h)
                spread[t, h, 0] = group(h, wrap(f + 2)).astype(BF)
                for q, far in enumerate((2, 1, -1, 0)):
                    to = wrap(s + far)
                    for n, d in both:
                        send(
                            base[h] + 2 * q + n, spread.at[t, h, 0, to, pl.ds(32 * n, 32)],
                            f_opp.at[t, h, q, n], fd[d],
                        )

        def e1():
            for h in range(2):
                f, s, fd, sd = axes(h)
                for n, d in both:
                    spread[t, h, 1 + n] = group(h, wrap(f + d)).astype(BF)

        def e2():
            for h in range(2):
                home[t, h] = group(h, axes(h)[0])

        def fn(q, far):
            def run():
                for h in range(2):
                    f, s, fd, sd = axes(h)
                    to = wrap(s + far)
                    for n, d in both:
                        recv(base[h] + 2 * q + n, f_opp.at[t, h, q, n], fd[d])
                        here = slice(32 * n, 32 * n + 32)
                        spread[t, h, 1 + n, to, here] = (
                            spread[t, h, 1 + n, to, here].astype(F32)
                            + f_opp[t, h, q, n].astype(F32)
                        ).astype(BF)
                        send(
                            base[h] + 8 + 2 * q + n, spread.at[t, h, 1 + n, to],
                            f_nbr.at[t, h, q, n], fd[d],
                        )
            return run

        def fs(q, far):
            def run():
                for h in range(2):
                    f, s, fd, sd = axes(h)
                    to = wrap(s + far)
                    for n, d in both:
                        recv(base[h] + 8 + 2 * q + n, f_nbr.at[t, h, q, n], fd[d])
                    got = (
                        home[t, h, to]
                        + f_nbr[t, h, q, 0].astype(F32)
                        + f_nbr[t, h, q, 1].astype(F32)
                    )
                    if q == 3:
                        home[t, h, to] = got
                    else:
                        grouped[t, h, q] = got.astype(BF)
                        send(
                            base[h] + 16 + q, grouped.at[t, h, q], s_rx.at[t, h, q], sd[far]
                        )
            return run

        def g3():
            for h in range(2):
                f, s, fd, sd = axes(h)
                got = home[t, h, s]
                for q, far in enumerate((2, 1, -1)):
                    recv(base[h] + 16 + q, s_rx.at[t, h, q], sd[far])
                    got = got + s_rx[t, h, q].astype(F32)
                if t == 0:
                    got = gate[:, 0:1] * got
                slots_out[t, :, 512 * h:512 * h + 512] = got.astype(BF)

        for f in (e0, e1, e2, g3):
            tasks[f"{f.__name__}_{t}"] = f
        for q, far in enumerate((2, 1, -1, 0)):
            tasks[f"fn{q}_{t}"] = fn(q, far)
            tasks[f"fs{q}_{t}"] = fs(q, far)

    def dwo_tile(j):
        def run():
            here = pl.ds(256 * j, 256)
            dwo[here, :] = dot(hb[0, :, here], rows[1], TN).astype(BF)
            local_copy(dwo.at[here], dwo_out.at[here])
        return run

    def dwi_tile(j):
        def run():
            here = pl.ds(256 * j, 256)
            dwi[here, :] = dot(rows[0, :, here], hb[1], TN).astype(BF)
            local_copy(dwi.at[here], dwi_out.at[here])
        return run

    for j in range(8):
        tasks[f"dwo{j}"] = dwo_tile(j)
    for j in range(4):
        tasks[f"dwi{j}"] = dwi_tile(j)
    for t in range(2):
        for i in range(2):
            add_gather(t, i)
            add_chunk(t, i)
        add_home(t)

    entered = False
    for name in ORDER:
        if name == "ag1_00":
            pl.semaphore_wait(barrier, len(partners))
            entered = True
        assert entered or name.startswith("pick")
        tasks.pop(name)()
    assert not tasks

    for d in sent:
        d.wait_send()
    for d in opened[4:]:
        d.wait()


def exchange(chosen, gates, counts, tokens, cotangent, w_in, w_out):
    vmem = pl.BlockSpec(memory_space=pltpu.VMEM)
    smem = pl.BlockSpec(memory_space=pltpu.SMEM)
    anywhere = pl.BlockSpec(memory_space=pl.ANY)

    def v(*shape, dtype=BF):
        return pltpu.VMEM(shape, dtype)

    return pl.pallas_call(
        kernel,
        out_shape=(
            jax.ShapeDtypeStruct((64, 256), BF),
            jax.ShapeDtypeStruct((2, 64, 1024), BF),
            jax.ShapeDtypeStruct((1024, 2048), BF),
            jax.ShapeDtypeStruct((2048, 1024), BF),
        ),
        in_specs=[vmem, vmem, smem] + [anywhere] * 4,
        out_specs=(vmem, vmem, anywhere, anywhere),
        scratch_shapes=[
            v(256, 1024), v(256, 1024), v(1024, 2048), v(2048, 1024),
            v(64, 128, dtype=F32),
            v(2, 2, 2, 4, 4, 32, 512),
            v(4, 4, 8, 128, dtype=jnp.int32),
            v(3, 256, 512),
            v(4, 4, 64, 512),
            v(2, 512, 1024),
            v(2, 2, 2, 2, 256, 256), v(2, 2, 2, 2, 256, 256),
            v(2, 2, 3, 256, 256),
            v(2, 2, 2, 128, 256),
            v(2, 2, 2, 256, 256),
            v(2, 2, 2, 2, 256, 256, dtype=F32),
            v(2, 256, 256, dtype=F32),
            v(2, 512, 2048),
            v(256, 1024, dtype=F32),
            v(2, 512, 1024),
            v(2, 2, 3, 4, 64, 512),
            v(2, 2, 4, 64, 512, dtype=F32),
            v(2, 2, 4, 2, 32, 512),
            v(2, 2, 4, 2, 64, 512),
            v(2, 2, 3, 64, 512),
            v(2, 2, 3, 64, 512),
            v(1024, 2048), v(2048, 1024),
            pltpu.SemaphoreType.DMA((N_COPIES,)),
            pltpu.SemaphoreType.DMA((N_COPIES,)),
            pltpu.SemaphoreType.DMA((N_LOCAL,)),
        ],
        compiler_params=pltpu.CompilerParams(
            collective_id=0, has_side_effects=True, vmem_limit_bytes=62 * 2**20
        ),
        cost_estimate=pl.CostEstimate(
            flops=14 * 10**9, bytes_accessed=20 * 2**20, transcendentals=2**19
        ),
    )(chosen, gates, counts, tokens, cotangent, w_in, w_out)


def local(tokens, w_in, w_out, chosen, counts, gates, cotangent):
    pick, slots, d_w_in, d_w_out = exchange(
        chosen, gates, counts, tokens, cotangent, w_in, w_out
    )

    def scatter(rows):
        return dot(pick, rows, TN).astype(BF)

    return scatter(slots[0]), scatter(slots[1]), d_w_in, d_w_out


def solution(mesh):
    in_specs = (
        P("dp", "expert"),
        P("expert", "dp"),
        P("dp", "expert"),
        P("dp", None),
        P("dp"),
        P("dp", None),
        P("dp", "expert"),
    )
    out_specs = (P("dp", "expert"), P("dp", "expert"), P("expert", "dp"), P("dp", "expert"))
    return jax.shard_map(local, mesh=mesh, in_specs=in_specs, out_specs=out_specs, check_vma=False)
```

```python
import jax
import jax.numpy as jnp
from jax import lax
from jax.experimental import pallas as pl
from jax.experimental.pallas import tpu as pltpu
from jax.sharding import PartitionSpec as P

half_root = 0.7071067811865476
inv_root_tau = 0.3989422804014327

MESH = pl.DeviceIdType.MESH
BF = jnp.bfloat16
F32 = jnp.float32

N_COPIES = 200
N_LOCAL = 24

ORDER = (
    "pick0", "ag1_00", "ag1_01", "pick1", "ag1_10", "meta1", "ag2_00", "ag2_01", "meta2",
    "ag3_00", "ag3_01", "ag1_11", "ag2_10", "meta", "buildc", "ag4_00", "cmp_00", "ma_00",
    "ag4_01", "mb_00", "cmp_01", "ma_01", "mc_00", "mb_01", "md_00", "nb_00", "ag3_10", "mc_01",
    "buildct", "ag2_11", "md_01", "nb_01", "fin_00", "ag3_11", "fin_01", "ag4_10", "cmp_10",
    "ma_10", "ag4_11", "cmp_11", "fwd_00", "ma_11", "mb_10", "mc_10", "mb_11", "mc_11", "fwd_01",
    "opp_00", "md_11", "md_10", "nb_10", "ct_00", "opp_01", "nb_11", "ct_01", "fin_10", "e0_0",
    "e1_0", "fin_11", "dwo0", "fn0_0", "fn1_0", "fwd_10", "e2_0", "dwo1", "fn2_0", "dwo2",
    "fn3_0", "fs0_0", "fwd_11", "fs1_0", "opp_10", "ct1_11", "fs2_0", "opp_11", "ct_10", "ct2_11",
    "e0_1", "e1_1", "fs3_0", "dwi0", "dwo3", "fn0_1", "dwo4", "fn1_1", "g3_0", "fn2_1", "dwo5",
    "dwo6", "fn3_1", "dwi1", "dwi2", "e2_1", "fs0_1", "fs1_1", "fs2_1", "fs3_1", "dwo7", "dwi3",
    "g3_1",
)

NN = (((1,), (0,)), ((), ()))
NT = (((1,), (1,)), ((), ()))
TN = (((0,), (0,)), ((), ()))


def dot(a, b, dims=NN):
    return lax.dot_general(a, b, dims, preferred_element_type=F32)


def gelu_pair(pre_act):
    cdf_part = 0.5 * (1.0 + lax.erf(pre_act * half_root))
    slopes = cdf_part + pre_act * jnp.exp(-0.5 * pre_act * pre_act) * inv_root_tau
    return (pre_act * cdf_part, slopes)


def wrap(v):
    return lax.rem(v + 8, 4)


def kernel(
    chosen_ref, gates_ref, count_ref, tok_hbm, cot_hbm, wi_hbm, wo_hbm,
    pick_out, slots_out, dwi_out, dwo_out,
    tok, cot, wi, wo, gate, ag, cnt, c_mat, ct, rows, xs, xr, ps, opp_rx, nbr_rx, acc, slope, hb,
    sub, part, spread, home, f_opp, f_nbr, grouped, s_rx, dwi, dwo,
    send_sem, recv_sem, local_sem,
):
    dp, ex = lax.axis_index("dp"), lax.axis_index("expert")
    x, z = lax.div(dp, 4), lax.rem(dp, 4)
    y, c = lax.div(ex, 2), lax.rem(ex, 2)
    oc = 1 - c
    dev_x = {d: (wrap(x + d) * 4 + z, ex) for d in (1, -1, 2)}
    dev_z = {d: (x * 4 + wrap(z + d), ex) for d in (1, -1, 2)}
    dev_y = {d: (dp, wrap(y + d) * 2 + c) for d in (1, -1)}
    dev_c = (dp, y * 2 + oc)
    both = ((0, 1), (1, -1))
    three = ((0, 1), (1, -1), (2, 2))

    counter = [0]
    sent = []

    def fresh(n):
        first = counter[0]
        counter[0] += n
        assert counter[0] <= N_COPIES
        return first

    def copy(i, src, dst, dev):
        return pltpu.make_async_remote_copy(
            src_ref=src, dst_ref=dst, send_sem=send_sem.at[i], recv_sem=recv_sem.at[i],
            device_id=dev, device_id_type=MESH,
        )

    def send(i, src, dst, dev):
        d = copy(i, src, dst, dev)
        d.start()
        sent.append(d)

    def recv(i, landing, dev):
        copy(i, landing, landing, dev).wait_recv()

    opened = []

    def local_copy(src, dst):
        d = pltpu.make_async_copy(src, dst, local_sem.at[len(opened)])
        d.start()
        opened.append(d)
        return d

    load = {
        "tok": local_copy(tok_hbm, tok),
        "cot": local_copy(cot_hbm, cot),
        0: local_copy(wi_hbm, wi),
        1: local_copy(wo_hbm, wo),
    }

    barrier = pltpu.get_barrier_semaphore()
    partners = [dev_x[d] for d in dev_x] + [dev_z[d] for d in dev_z] + [dev_y[1], dev_y[-1], dev_c]
    for dev in partners:
        pl.semaphore_signal(barrier, inc=1, device_id=dev, device_id_type=MESH)

    tasks = {}

    def column(row):
        here = lax.broadcasted_iota(jnp.int32, (64, 64), 0)
        there = lax.broadcasted_iota(jnp.int32, (64, 64), 1)
        wide = jnp.broadcast_to(row.astype(F32), (64, 64))
        return jnp.sum(jnp.where(here == there, wide, 0.0), axis=1, keepdims=True)

    def pick0():
        place = jnp.broadcast_to(column(chosen_ref[...]), (64, 256)).astype(jnp.int32)
        spot = lax.broadcasted_iota(jnp.int32, (64, 256), 1)
        slot = lax.broadcasted_iota(jnp.int32, (64, 256), 0)
        held = jnp.broadcast_to(count_ref[0], (64, 256))
        hit = jnp.where(place == spot, 1.0, 0.0) * jnp.where(slot < held, 1.0, 0.0)
        pick_out[...] = hit.astype(BF)
        gate[...] = jnp.broadcast_to(column(gates_ref[...]), (64, 128))
        cnt[x, z] = jnp.broadcast_to(count_ref[0], (8, 128))
        load["tok"].wait()
        keep(0, dot(pick_out[...], tok[...]).astype(BF))

    def pick1():
        load["cot"].wait()
        keep(1, (gate[:, 0:1] * dot(pick_out[...], cot[...])).astype(BF))

    def keep(t, got):
        for ph in range(2):
            for h in range(2):
                ag[t, ph, h, x, z] = got[32 * ph:32 * ph + 32, 512 * h:512 * h + 512]

    tasks["pick0"], tasks["pick1"] = pick0, pick1

    def axes(h):
        return (x, z, dev_x, dev_z) if h == 0 else (z, x, dev_z, dev_x)

    def add_gather(t, ph):
        base = [fresh(7), fresh(7)]

        def blk(h, fi, si):
            return ag.at[(t, ph, h) + ((fi, si) if h == 0 else (si, fi))]

        def grp(h, si, first, n):
            many = pl.ds(first, n)
            return ag.at[(t, ph, h) + ((many, si) if h == 0 else (si, many))]

        def ag1():
            for h in range(2):
                f, s, fd, sd = axes(h)
                for n, d in three:
                    send(base[h] + n, blk(h, f, s), blk(h, f, s), fd[d])

        def ag2():
            for h in range(2):
                f, s, fd, sd = axes(h)
                for n, d in three:
                    recv(base[h] + n, blk(h, wrap(f - d), s), fd[d])
                for n, d in both:
                    send(base[h] + 3 + n, grp(h, s, 0, 4), grp(h, s, 0, 4), sd[d])

        def ag3():
            for h in range(2):
                f, s, fd, sd = axes(h)
                for n, d in both:
                    recv(base[h] + 3 + n, grp(h, wrap(s - d), 0, 4), sd[d])
                    g = grp(h, wrap(s - d), 2 * n, 2)
                    send(base[h] + 5 + n, g, g, sd[d])

        def ag4():
            for h in range(2):
                f, s, fd, sd = axes(h)
                for n, d in both:
                    recv(base[h] + 5 + n, grp(h, wrap(s + 2), 2 * n, 2), sd[d])

        for name, f in (("ag1", ag1), ("ag2", ag2), ("ag3", ag3), ("ag4", ag4)):
            tasks[f"{name}_{t}{ph}"] = f

    meta_base = fresh(6)

    def meta1():
        for n, d in three:
            send(meta_base + n, cnt.at[x, z], cnt.at[x, z], dev_x[d])

    def meta2():
        for n, d in three:
            recv(meta_base + n, cnt.at[wrap(x - d), z], dev_x[d])
        for n, d in three:
            send(meta_base + 3 + n, cnt.at[:, z], cnt.at[:, z], dev_z[d])

    def meta():
        for n, d in three:
            recv(meta_base + 3 + n, cnt.at[:, wrap(z - d)], dev_z[d])

    tasks.update(meta1=meta1, meta2=meta2, meta=meta)

    def places():
        first, second = [], []
        total = jnp.zeros((8, 128), jnp.int32)
        for i in range(16):
            held = jnp.minimum(cnt[i // 4, i % 4], 32)
            first.append((total, held))
            total = total + held
        for i in range(16):
            held = jnp.maximum(cnt[i // 4, i % 4] - 32, 0)
            second.append((total, held))
            total = total + held
        return first, second

    def lane_places(shards):
        lane = lax.broadcasted_iota(jnp.int32, (8, 128), 1)
        quarter, slot = lane // 32, lane % 32
        tiles = []
        for b in range(4):
            start, held = shards[4 * b + 3]
            for j in (2, 1, 0):
                start = jnp.where(quarter == j, shards[4 * b + j][0], start)
                held = jnp.where(quarter == j, shards[4 * b + j][1], held)
            tiles.append(jnp.where(slot < held, start + slot, -1))
        return tiles

    def buildc():
        first, second = places()
        row = lax.broadcasted_iota(jnp.int32, (256, 128), 0)
        for n, (shards, k) in enumerate(((first, 0), (first, 1), (second, 1))):
            for b, tile in enumerate(lane_places(shards)):
                hit = jnp.broadcast_to(tile[0:1], (256, 128)) == row + 256 * k
                c_mat[n, :, 128 * b:128 * b + 128] = jnp.where(hit, 1.0, 0.0).astype(BF)

    def buildct():
        first, second = places()
        slot = lax.broadcasted_iota(jnp.int32, (32, 128), 0)
        lane = lax.broadcasted_iota(jnp.int32, (32, 128), 1)
        for i in range(16):
            for ph, shards in ((0, first), (1, second)):
                start = jnp.broadcast_to(shards[i][0][0:1], (32, 128))
                held = jnp.broadcast_to(shards[i][1][0:1], (32, 128))
                place = jnp.where(slot < held, start + slot, -1)
                for b in range(4):
                    hit = place == lane + 128 * b
                    ct[i // 4, i % 4, 32 * ph:32 * ph + 32, 128 * b:128 * b + 128] = jnp.where(
                        hit, 1.0, 0.0
                    ).astype(BF)

    tasks["buildc"], tasks["buildct"] = buildc, buildct

    def hidden_cols(core, yy, width=256):
        return pl.ds(pl.multiple_of(core * 1024 + yy * width, width), width)

    def add_chunk(t, k):
        mine = pl.ds(256 * k, 256)
        ic, io, inb = fresh(2), fresh(2), fresh(2)
        iy, iw, ih = fresh(2), fresh(2), fresh(4)
        far = lax.div(wrap(y + 2), 2)
        near = 1 - far

        def cmp():
            for h in range(2):
                cols = slice(512 * h, 512 * h + 512)
                got = dot(c_mat[k], ag[t, 0, h].reshape(512, 512))
                if k == 1:
                    got += dot(c_mat[2], ag[t, 1, h].reshape(512, 512))
                rows[t, mine, cols] = got.astype(BF)

        def pair(core, p):
            left = rows[t, mine, :]
            if t == 0:
                return dot(left, wi[:, hidden_cols(core, p, 512)])
            return dot(left, wo[hidden_cols(core, p, 512), :], NT)

        def for_other(p, n):
            got = pair(oc, p).astype(BF)
            xs[t, k, p, 0] = got[:, :256]
            xs[t, k, p, 1] = got[:, 256:]
            send(ic + n, xs.at[t, k, p], xr.at[t, k, p], dev_c)

        def for_self(p, n):
            got = pair(c, p)
            recv(ic + n, xr.at[t, k, p], dev_c)
            acc[t, k, p, 0] = got[:, :256] + xr[t, k, p, 0].astype(F32)
            acc[t, k, p, 1] = got[:, 256:] + xr[t, k, p, 1].astype(F32)

        def tile(yy):
            return (t, k, lax.div(yy, 2), lax.rem(yy, 2))

        def ma():
            if k == 0:
                load[t].wait()
            for_other(far, 0)

        def mb():
            for_self(far, 0)
            ps[t, k, 0] = acc[tile(wrap(y + 2))].astype(BF)
            for n, d in both:
                send(io + n, ps.at[t, k, 0, pl.ds(128 * n, 128)], opp_rx.at[t, k, n], dev_y[d])

        def mc():
            for_other(near, 1)

        def md():
            for_self(near, 1)

        def nb():
            for n, d in both:
                recv(io + n, opp_rx.at[t, k, n], dev_y[d])
                got = acc[tile(wrap(y + d))]
                here = slice(128 * n, 128 * n + 128)
                away = slice(128 - 128 * n, 256 - 128 * n)
                ps[t, k, 1 + n, here] = (got[here] + opp_rx[t, k, n].astype(F32)).astype(BF)
                ps[t, k, 1 + n, away] = got[away].astype(BF)
                send(inb + n, ps.at[t, k, 1 + n], nbr_rx.at[t, k, n], dev_y[d])

        def piece(core, yy):
            return hb.at[t, mine, hidden_cols(core, yy)]

        def half(yy, n):
            return hb.at[t, pl.ds(256 * k + 128 * n, 128), hidden_cols(c, yy)]

        def fin():
            for n, d in both:
                recv(inb + n, nbr_rx.at[t, k, n], dev_y[d])
            total = acc[tile(y)] + nbr_rx[t, k, 0].astype(F32) + nbr_rx[t, k, 1].astype(F32)
            if t == 0:
                total, slopes = gelu_pair(total)
                slope[k] = slopes
            else:
                total = total * slope[k]
            hb[t, mine, hidden_cols(c, y)] = total.astype(BF)
            p = piece(c, y)
            send(iy, p, p, dev_y[1])
            send(iy + 1, p, p, dev_y[-1])
            send(ih, p, p, dev_c)

        def fwd():
            for n, d in both:
                p, q = piece(c, wrap(y - d)), half(wrap(y - d), n)
                recv(iy + n, p, dev_y[d])
                send(iw + n, q, q, dev_y[d])
                send(ih + 1 + n, p, p, dev_c)

        def opp():
            for n, d in both:
                recv(iw + n, half(wrap(y + 2), n), dev_y[d])
            p = piece(c, wrap(y + 2))
            send(ih + 3, p, p, dev_c)

        def near_in():
            for n, yy in enumerate((y, wrap(y - 1), wrap(y + 1))):
                recv(ih + n, piece(oc, yy), dev_c)

        def far_in():
            recv(ih + 3, piece(oc, wrap(y + 2)), dev_c)

        def whole():
            near_in()
            far_in()

            def step(n, carry):
                cols = pl.ds(pl.multiple_of(n * 256, 256), 256)
                left = hb[t, mine, :]
                got = dot(left, wo[:, cols]) if t == 0 else dot(left, wi[cols, :], NT)
                part[t, mine, cols] = got.astype(BF)
                return carry

            lax.fori_loop(0, 4, step, 0)

        def product(core, yy):
            units = hidden_cols(core, yy)
            left = hb[t, mine, units]
            return dot(left, wo[units, :]) if t == 0 else dot(left, wi[:, units], NT)

        def ct1():
            near_in()
            sub[...] = product(c, y)

            def step(n, carry):
                sub[...] += product(lax.rem(c + lax.div(n, 3), 2), wrap(y + 3 + lax.rem(n, 3)))
                return carry

            lax.fori_loop(0, 1, lambda n, carry: step(2, carry), 0)
            lax.fori_loop(3, 6, step, 0)
            lax.fori_loop(0, 1, step, 0)

        def ct2():
            far_in()
            got = sub[...] + product(c, wrap(y + 2)) + product(oc, wrap(y + 2))
            part[t, mine, :] = got.astype(BF)

        for f in (cmp, ma, mb, mc, md, nb, fin, fwd, opp):
            tasks[f"{f.__name__}_{t}{k}"] = f
        if (t, k) == (1, 1):
            tasks["ct1_11"], tasks["ct2_11"] = ct1, ct2
        else:
            tasks[f"ct_{t}{k}"] = whole

    def add_home(t):
        base = [fresh(19), fresh(19)]

        def group(h, fi):
            picks = ct[fi] if h == 0 else ct[:, fi]
            got = dot(picks.reshape(256, 512), part[t, :, 512 * h:512 * h + 512])
            return got.reshape(4, 64, 512)

        def e0():
            for h in range(2):
                f, s, fd, sd = axes(h)
                spread[t, h, 0] = group(h, wrap(f + 2)).astype(BF)
                for q, far in enumerate((2, 1, -1, 0)):
                    to = wrap(s + far)
                    for n, d in both:
                        send(
                            base[h] + 2 * q + n, spread.at[t, h, 0, to, pl.ds(32 * n, 32)],
                            f_opp.at[t, h, q, n], fd[d],
                        )

        def e1():
            for h in range(2):
                f, s, fd, sd = axes(h)
                for n, d in both:
                    spread[t, h, 1 + n] = group(h, wrap(f + d)).astype(BF)

        def e2():
            for h in range(2):
                home[t, h] = group(h, axes(h)[0])

        def fn(q, far):
            def run():
                for h in range(2):
                    f, s, fd, sd = axes(h)
                    to = wrap(s + far)
                    for n, d in both:
                        recv(base[h] + 2 * q + n, f_opp.at[t, h, q, n], fd[d])
                        here = slice(32 * n, 32 * n + 32)
                        spread[t, h, 1 + n, to, here] = (
                            spread[t, h, 1 + n, to, here].astype(F32)
                            + f_opp[t, h, q, n].astype(F32)
                        ).astype(BF)
                        send(
                            base[h] + 8 + 2 * q + n, spread.at[t, h, 1 + n, to],
                            f_nbr.at[t, h, q, n], fd[d],
                        )
            return run

        def fs(q, far):
            def run():
                for h in range(2):
                    f, s, fd, sd = axes(h)
                    to = wrap(s + far)
                    for n, d in both:
                        recv(base[h] + 8 + 2 * q + n, f_nbr.at[t, h, q, n], fd[d])
                    got = (
                        home[t, h, to]
                        + f_nbr[t, h, q, 0].astype(F32)
                        + f_nbr[t, h, q, 1].astype(F32)
                    )
                    if q == 3:
                        home[t, h, to] = got
                    else:
                        grouped[t, h, q] = got.astype(BF)
                        send(
                            base[h] + 16 + q, grouped.at[t, h, q], s_rx.at[t, h, q], sd[far]
                        )
            return run

        def g3():
            for h in range(2):
                f, s, fd, sd = axes(h)
                got = home[t, h, s]
                for q, far in enumerate((2, 1, -1)):
                    recv(base[h] + 16 + q, s_rx.at[t, h, q], sd[far])
                    got = got + s_rx[t, h, q].astype(F32)
                if t == 0:
                    got = gate[:, 0:1] * got
                slots_out[t, :, 512 * h:512 * h + 512] = got.astype(BF)

        for f in (e0, e1, e2, g3):
            tasks[f"{f.__name__}_{t}"] = f
        for q, far in enumerate((2, 1, -1, 0)):
            tasks[f"fn{q}_{t}"] = fn(q, far)
            tasks[f"fs{q}_{t}"] = fs(q, far)

    moved = {}

    def dwo_tile(j):
        def run():
            here = pl.ds(256 * j, 256)
            got = dot(hb[0, :, here], rows[1], TN).astype(BF)
            if j >= 2:
                moved["o", j - 2].wait()
            dwo[j % 2] = got
            moved["o", j] = local_copy(dwo.at[j % 2], dwo_out.at[here])
        return run

    def dwi_tile(j):
        def run():
            here = pl.ds(256 * j, 256)
            got = dot(rows[0, :, here], hb[1], TN).astype(BF)
            if j >= 2:
                moved["i", j - 2].wait()
            dwi[j % 2] = got
            moved["i", j] = local_copy(dwi.at[j % 2], dwi_out.at[here])
        return run

    for j in range(8):
        tasks[f"dwo{j}"] = dwo_tile(j)
    for j in range(4):
        tasks[f"dwi{j}"] = dwi_tile(j)
    for t in range(2):
        for i in range(2):
            add_gather(t, i)
            add_chunk(t, i)
        add_home(t)

    entered = False
    for name in ORDER:
        if name == "ag1_00":
            pl.semaphore_wait(barrier, len(partners))
            entered = True
        assert entered or name.startswith("pick")
        tasks.pop(name)()
    assert not tasks

    for d in sent:
        d.wait_send()
    for j in (6, 7):
        moved["o", j].wait()
    for j in (2, 3):
        moved["i", j].wait()


def exchange(chosen, gates, counts, tokens, cotangent, w_in, w_out):
    vmem = pl.BlockSpec(memory_space=pltpu.VMEM)
    smem = pl.BlockSpec(memory_space=pltpu.SMEM)
    anywhere = pl.BlockSpec(memory_space=pl.ANY)
    hbm = pl.BlockSpec(memory_space=pltpu.HBM)

    def v(*shape, dtype=BF):
        return pltpu.VMEM(shape, dtype)

    return pl.pallas_call(
        kernel,
        out_shape=(
            pltpu.VMEM((64, 256), BF),
            pltpu.VMEM((2, 64, 1024), BF),
            pltpu.VMEM((1024, 2048), BF),
            pltpu.VMEM((2048, 1024), BF),
        ),
        in_specs=[vmem, vmem, smem] + [hbm] * 4,
        out_specs=(vmem, vmem, anywhere, anywhere),
        scratch_shapes=[
            v(256, 1024), v(256, 1024), v(1024, 2048), v(2048, 1024),
            v(64, 128, dtype=F32),
            v(2, 2, 2, 4, 4, 32, 512),
            v(4, 4, 8, 128, dtype=jnp.int32),
            v(3, 256, 512),
            v(4, 4, 64, 512),
            v(2, 512, 1024),
            v(2, 2, 2, 2, 256, 256), v(2, 2, 2, 2, 256, 256),
            v(2, 2, 3, 256, 256),
            v(2, 2, 2, 128, 256),
            v(2, 2, 2, 256, 256),
            v(2, 2, 2, 2, 256, 256, dtype=F32),
            v(2, 256, 256, dtype=F32),
            v(2, 512, 2048),
            v(256, 1024, dtype=F32),
            v(2, 512, 1024),
            v(2, 2, 3, 4, 64, 512),
            v(2, 2, 4, 64, 512, dtype=F32),
            v(2, 2, 4, 2, 32, 512),
            v(2, 2, 4, 2, 64, 512),
            v(2, 2, 3, 64, 512),
            v(2, 2, 3, 64, 512),
            v(2, 256, 2048), v(2, 256, 1024),
            pltpu.SemaphoreType.DMA((N_COPIES,)),
            pltpu.SemaphoreType.DMA((N_COPIES,)),
            pltpu.SemaphoreType.DMA((N_LOCAL,)),
        ],
        compiler_params=pltpu.CompilerParams(
            collective_id=0, has_side_effects=True, vmem_limit_bytes=54 * 2**20
        ),
        cost_estimate=pl.CostEstimate(
            flops=14 * 10**9, bytes_accessed=20 * 2**20, transcendentals=2**19
        ),
    )(chosen, gates, counts, tokens, cotangent, w_in, w_out)


def finish_kernel(
    pick_ref, slots_ref, dwi_in, dwo_in, mixed_ref, d_tok_ref, dwi_out, dwo_out, sem
):
    moves = []
    for src, dst, n in ((dwi_in, dwi_out, 256), (dwo_in, dwo_out, 512)):
        for j in range(4):
            here = pl.ds(n * j, n)
            d = pltpu.make_async_copy(src.at[here], dst.at[here], sem.at[len(moves)])
            d.start()
            moves.append(d)
    mixed_ref[...] = dot(pick_ref[...], slots_ref[0], TN).astype(BF)
    d_tok_ref[...] = dot(pick_ref[...], slots_ref[1], TN).astype(BF)
    for d in moves:
        d.wait()


def finish(pick, slots, d_w_in, d_w_out):
    vmem = pl.BlockSpec(memory_space=pltpu.VMEM)
    anywhere = pl.BlockSpec(memory_space=pl.ANY)
    hbm = pl.BlockSpec(memory_space=pltpu.HBM)
    return pl.pallas_call(
        finish_kernel,
        out_shape=(
            jax.ShapeDtypeStruct((256, 1024), BF),
            jax.ShapeDtypeStruct((256, 1024), BF),
            jax.ShapeDtypeStruct((1024, 2048), BF),
            jax.ShapeDtypeStruct((2048, 1024), BF),
        ),
        in_specs=[vmem, vmem, anywhere, anywhere],
        out_specs=(vmem, vmem, hbm, hbm),
        scratch_shapes=[pltpu.SemaphoreType.DMA((8,))],
        compiler_params=pltpu.CompilerParams(vmem_limit_bytes=8 * 2**20),
        cost_estimate=pl.CostEstimate(
            flops=6 * 10**7, bytes_accessed=18 * 2**20, transcendentals=0
        ),
    )(pick, slots, d_w_in, d_w_out)


def local(tokens, w_in, w_out, chosen, counts, gates, cotangent):
    return finish(*exchange(chosen, gates, counts, tokens, cotangent, w_in, w_out))


def solution(mesh):
    in_specs = (
        P("dp", "expert"),
        P("expert", "dp"),
        P("dp", "expert"),
        P("dp", None),
        P("dp"),
        P("dp", None),
        P("dp", "expert"),
    )
    out_specs = (P("dp", "expert"), P("dp", "expert"), P("expert", "dp"), P("dp", "expert"))
    return jax.shard_map(local, mesh=mesh, in_specs=in_specs, out_specs=out_specs, check_vma=False)
```

```python
import jax
import jax.numpy as jnp
from jax import lax
from jax.experimental import pallas as pl
from jax.experimental.pallas import tpu as pltpu
from jax.sharding import PartitionSpec as P

half_root = 0.7071067811865476
inv_root_tau = 0.3989422804014327

MESH = pl.DeviceIdType.MESH
BF = jnp.bfloat16
F32 = jnp.float32

N_COPIES = 300
N_LOCAL = 24

CHUNKS = ([(0, 128), (128, 128), (256, 128), (384, 128)], [(0, 256), (256, 256)])
PHASES = ([(0, 1), (1, 1), (2, 1), (3, 1)], [(0, 2), (2, 2)])

ORDER = (
    "pick0", "ag1_00", "meta1", "ag1_01", "ag1_02", "ag1_03", "meta2", "ag2_01", "ag2_00", "meta",
    "ag3_01", "buildct", "ag2_02", "ag2_03", "buildc0", "buildc1", "pick1", "ag1_10", "ag3_00",
    "ag4_01", "ag4_00", "cmp_01", "ma_01", "cmp_00", "ma_00", "mb_01", "ag3_02", "mc_01", "mb_00",
    "ag3_03", "mc_00", "md_01", "ag1_11", "md_00", "nb_01", "ag2_10", "ag4_02", "cmp_02", "ma_02",
    "nb_00", "ag4_03", "cmp_03", "ma_03", "mb_02", "mc_02", "mb_03", "ag2_11", "fin_01", "md_02",
    "mc_03", "fin_00", "nb_02", "ag3_10", "md_03", "nb_03", "fwd_00", "ag3_11", "fwd_01",
    "ag4_10", "cmp_10", "fin_02", "ma_10", "fin_03", "mb_10", "ag4_11", "cmp_11", "ma_11",
    "mc_10", "fwd_02", "opp_00", "mb_11", "mc_11", "opp_01", "fwd_03", "md_10", "nb_10", "md_11",
    "opp_02", "ct_00", "opp_03", "nb_11", "ct_01", "fin_10", "e0_m", "dwo0", "e1_m", "fin_11",
    "fn0_m", "fn1_m", "dwo1", "fwd_10", "fn2_m", "e2_m", "dwo2", "dwo3", "fwd_11", "fn3_m",
    "fs0_m", "fs1_m", "opp_10", "ct1_11", "fs2_m", "opp_11", "ct_10", "ct2_11", "e0_d1", "e1_d1",
    "dwo4", "dwi0", "fn0_d1", "fn1_d1", "fn2_d1", "dwo5", "dwi1", "e2_d1", "fn3_d1", "fs0_d1",
    "fs3_m", "dwo6", "fs1_d1", "dwi2", "fs2_d1", "fs3_d1", "dwi3", "g3_m", "dwo7", "g3_d1",
)

NN = (((1,), (0,)), ((), ()))
NT = (((1,), (1,)), ((), ()))
TN = (((0,), (0,)), ((), ()))


def dot(a, b, dims=NN):
    return lax.dot_general(a, b, dims, preferred_element_type=F32)


def gelu_pair(pre_act):
    cdf_part = 0.5 * (1.0 + lax.erf(pre_act * half_root))
    slopes = cdf_part + pre_act * jnp.exp(-0.5 * pre_act * pre_act) * inv_root_tau
    return (pre_act * cdf_part, slopes)


def wrap(v):
    return lax.rem(v + 8, 4)


def kernel(
    chosen_ref, gates_ref, count_ref, tok_hbm, cot_hbm, wi_hbm, wo_hbm,
    pick_out, slots_out, dwi_out, dwo_out,
    tok, cot, wi, wo, gate, ag, cnt, c_low, c_high, ct, rows, xs, xr, ps, opp_rx, nbr_rx, acc, slope, hb,
    sub, part, spread, home, f_opp, f_nbr, grouped, s_rx, dwi, dwo,
    send_sem, recv_sem, local_sem,
):
    dp, ex = lax.axis_index("dp"), lax.axis_index("expert")
    x, z = lax.div(dp, 4), lax.rem(dp, 4)
    y, c = lax.div(ex, 2), lax.rem(ex, 2)
    oc = 1 - c
    dev_x = {d: (wrap(x + d) * 4 + z, ex) for d in (1, -1, 2)}
    dev_z = {d: (x * 4 + wrap(z + d), ex) for d in (1, -1, 2)}
    dev_y = {d: (dp, wrap(y + d) * 2 + c) for d in (1, -1)}
    dev_c = (dp, y * 2 + oc)
    both = ((0, 1), (1, -1))
    three = ((0, 1), (1, -1), (2, 2))

    counter = [0]
    sent = []

    def fresh(n):
        first = counter[0]
        counter[0] += n
        assert counter[0] <= N_COPIES
        return first

    def copy(i, src, dst, dev):
        return pltpu.make_async_remote_copy(
            src_ref=src, dst_ref=dst, send_sem=send_sem.at[i], recv_sem=recv_sem.at[i],
            device_id=dev, device_id_type=MESH,
        )

    def send(i, src, dst, dev):
        d = copy(i, src, dst, dev)
        d.start()
        sent.append(d)

    def recv(i, landing, dev):
        copy(i, landing, landing, dev).wait_recv()

    opened = []

    def local_copy(src, dst):
        d = pltpu.make_async_copy(src, dst, local_sem.at[len(opened)])
        d.start()
        opened.append(d)
        return d

    load = {
        "tok": local_copy(tok_hbm, tok),
        "cot": local_copy(cot_hbm, cot),
        0: local_copy(wi_hbm, wi),
        1: local_copy(wo_hbm, wo),
    }

    barrier = pltpu.get_barrier_semaphore()
    partners = [dev_x[d] for d in dev_x] + [dev_z[d] for d in dev_z] + [dev_y[1], dev_y[-1], dev_c]
    for dev in partners:
        pl.semaphore_signal(barrier, inc=1, device_id=dev, device_id_type=MESH)

    tasks = {}

    def column(row):
        here = lax.broadcasted_iota(jnp.int32, (64, 64), 0)
        there = lax.broadcasted_iota(jnp.int32, (64, 64), 1)
        wide = jnp.broadcast_to(row.astype(F32), (64, 64))
        return jnp.sum(jnp.where(here == there, wide, 0.0), axis=1, keepdims=True)

    def pick0():
        place = jnp.broadcast_to(column(chosen_ref[...]), (64, 256)).astype(jnp.int32)
        spot = lax.broadcasted_iota(jnp.int32, (64, 256), 1)
        slot = lax.broadcasted_iota(jnp.int32, (64, 256), 0)
        held = jnp.broadcast_to(count_ref[...], (64, 256))
        hit = jnp.where(place == spot, 1.0, 0.0) * jnp.where(slot < held, 1.0, 0.0)
        pick_out[...] = hit.astype(BF)
        gate[...] = jnp.broadcast_to(column(gates_ref[...]), (64, 128))
        cnt[x, z] = jnp.broadcast_to(count_ref[...], (8, 128))
        load["tok"].wait()
        keep(0, dot(pick_out[...], tok[...]).astype(BF))

    def pick1():
        load["cot"].wait()
        keep(1, (gate[:, 0:1] * dot(pick_out[...], cot[...])).astype(BF))

    def keep(t, got):
        for b in range(4):
            for h in range(2):
                ag[t, h, b, x, z] = got[16 * b:16 * b + 16, 512 * h:512 * h + 512]

    tasks["pick0"], tasks["pick1"] = pick0, pick1

    def axes(h):
        return (x, z, dev_x, dev_z) if h == 0 else (z, x, dev_z, dev_x)

    def add_gather(t, ph, b0, nb):
        base = [fresh(8), fresh(8)]
        blocks = pl.ds(b0, nb)
        direct = (t, ph) == (0, 0)

        def blk(h, fi, si):
            return ag.at[(t, h, blocks) + ((fi, si) if h == 0 else (si, fi))]

        def grp(h, si, first, n):
            many = pl.ds(first, n)
            return ag.at[(t, h, blocks) + ((many, si) if h == 0 else (si, many))]

        def ag1():
            for h in range(2):
                f, s, fd, sd = axes(h)
                for n, d in three:
                    send(base[h] + n, blk(h, f, s), blk(h, f, s), fd[d])

        def ag2():
            for h in range(2):
                f, s, fd, sd = axes(h)
                for n, d in three:
                    recv(base[h] + n, blk(h, wrap(f - d), s), fd[d])
                for n, d in three if direct else both:
                    send(base[h] + 3 + n, grp(h, s, 0, 4), grp(h, s, 0, 4), sd[d])

        def ag3():
            for h in range(2):
                f, s, fd, sd = axes(h)
                for n, d in three if direct else both:
                    recv(base[h] + 3 + n, grp(h, wrap(s - d), 0, 4), sd[d])
                    if not direct:
                        g = grp(h, wrap(s - d), 2 * n, 2)
                        send(base[h] + 6 + n, g, g, sd[d])

        def ag4():
            for h in range(2):
                f, s, fd, sd = axes(h)
                for n, d in both:
                    if not direct:
                        recv(base[h] + 6 + n, grp(h, wrap(s + 2), 2 * n, 2), sd[d])

        for name, f in (("ag1", ag1), ("ag2", ag2), ("ag3", ag3), ("ag4", ag4)):
            tasks[f"{name}_{t}{ph}"] = f

    meta_base = fresh(6)

    def meta1():
        for n, d in three:
            send(meta_base + n, cnt.at[x, z], cnt.at[x, z], dev_x[d])

    def meta2():
        for n, d in three:
            recv(meta_base + n, cnt.at[wrap(x - d), z], dev_x[d])
        for n, d in three:
            send(meta_base + 3 + n, cnt.at[:, z], cnt.at[:, z], dev_z[d])

    def meta():
        for n, d in three:
            recv(meta_base + 3 + n, cnt.at[:, wrap(z - d)], dev_z[d])

    tasks.update(meta1=meta1, meta2=meta2, meta=meta)

    def places(upto):
        total = jnp.zeros((8, 128), jnp.int32)
        found = []
        for b in range(upto):
            found.append([])
            for i in range(16):
                held = jnp.clip(cnt[i // 4, i % 4] - 16 * b, 0, 16)
                found[b].append((total, held))
                total = total + held
        return found

    def build_c(out, blocks, first_row):
        found = places(blocks[-1] + 1)
        lane = lax.broadcasted_iota(jnp.int32, (8, 128), 1)
        part_of, slot = lane // 16, lane % 16
        row = lax.broadcasted_iota(jnp.int32, (256, 128), 0) + first_row
        for b in blocks:
            for j in range(2):
                start, held = found[b][8 * j]
                for i in range(1, 8):
                    start = jnp.where(part_of == i, found[b][8 * j + i][0], start)
                    held = jnp.where(part_of == i, found[b][8 * j + i][1], held)
                place = jnp.where(slot < held, start + slot, -1)
                hit = jnp.broadcast_to(place[0:1], (256, 128)) == row
                at = 256 * (b - blocks[0]) + 128 * j
                out[:, at:at + 128] = jnp.where(hit, 1.0, 0.0).astype(BF)

    def buildc0():
        build_c(c_low, (0, 1), 0)

    def buildc1():
        build_c(c_high, (1, 2, 3), 256)

    def buildct():
        found = places(4)
        slot = lax.broadcasted_iota(jnp.int32, (16, 128), 0)
        lane = lax.broadcasted_iota(jnp.int32, (16, 128), 1)
        for i in range(16):
            for b in range(4):
                start = jnp.broadcast_to(found[b][i][0][0:1], (16, 128))
                held = jnp.broadcast_to(found[b][i][1][0:1], (16, 128))
                place = jnp.where(slot < held, start + slot, -1)
                for j in range(4):
                    hit = place == lane + 128 * j
                    ct[i // 4, i % 4, 16 * b:16 * b + 16, 128 * j:128 * j + 128] = jnp.where(
                        hit, 1.0, 0.0
                    ).astype(BF)

    tasks.update(buildc0=buildc0, buildc1=buildc1, buildct=buildct)

    def hidden_cols(core, yy, width=256):
        return pl.ds(pl.multiple_of(core * 1024 + yy * width, width), width)

    loaded = set()
    incoming = {}

    def add_chunk(t, k, r0, nr):
        mine = pl.ds(r0, nr)
        hr = nr // 2
        ic, io, inb = fresh(2), fresh(2), fresh(2)
        iy, iw, ih = fresh(2), fresh(2), fresh(4)
        far = lax.div(wrap(y + 2), 2)
        near = 1 - far

        def cmp():
            b0, b1 = (0 if r0 < 256 else 1), (r0 + nr) // 128
            width = 256 * (b1 - b0)
            at = r0 % 256
            picks = (c_low if r0 < 256 else c_high)[at:at + nr, :width]
            for h in range(2):
                got = dot(picks, ag[t, h, b0:b1].reshape(width, 512))
                rows[t, mine, 512 * h:512 * h + 512] = got.astype(BF)

        def pair(core, p):
            left = rows[t, mine, :]
            if t == 0:
                return dot(left, wi[:, hidden_cols(core, p, 512)])
            return dot(left, wo[hidden_cols(core, p, 512), :], NT)

        def for_other(p, n):
            got = pair(oc, p).astype(BF)
            xs[t, p, 0, mine] = got[:, :256]
            xs[t, p, 1, mine] = got[:, 256:]
            tiles = pl.ds(0, 2)
            send(ic + n, xs.at[t, p, tiles, mine], xr.at[t, p, tiles, mine], dev_c)

        def for_self(p, n):
            got = pair(c, p)
            recv(ic + n, xr.at[t, p, pl.ds(0, 2), mine], dev_c)
            acc[t, p, 0, mine] = got[:, :256] + xr[t, p, 0, mine].astype(F32)
            acc[t, p, 1, mine] = got[:, 256:] + xr[t, p, 1, mine].astype(F32)

        def tile(yy):
            return (t, lax.div(yy, 2), lax.rem(yy, 2), mine)

        def ma():
            if t not in loaded:
                loaded.add(t)
                load[t].wait()
            for_other(far, 0)

        def opp_landing(n):
            return (t, n, pl.ds(r0 // 2, hr))

        def mb():
            for_self(far, 0)
            ps[t, 0, mine] = acc[tile(wrap(y + 2))].astype(BF)
            for n, d in both:
                send(
                    io + n, ps.at[t, 0, pl.ds(r0 + hr * n, hr)], opp_rx.at[opp_landing(n)],
                    dev_y[d],
                )

        def mc():
            for_other(near, 1)

        def md():
            for_self(near, 1)

        def nb():
            for n, d in both:
                recv(io + n, opp_rx.at[opp_landing(n)], dev_y[d])
                got = acc[tile(wrap(y + d))]
                here = slice(hr * n, hr * n + hr)
                away = slice(hr - hr * n, nr - hr * n)
                added = got[here] + opp_rx[opp_landing(n)].astype(F32)
                ps[t, 1 + n, pl.ds(r0 + here.start, hr)] = added.astype(BF)
                ps[t, 1 + n, pl.ds(r0 + away.start, hr)] = got[away].astype(BF)
                send(inb + n, ps.at[t, 1 + n, mine], nbr_rx.at[t, n, mine], dev_y[d])

        def piece(core, yy):
            return hb.at[t, mine, hidden_cols(core, yy)]

        def half(yy, n):
            return hb.at[t, pl.ds(r0 + hr * n, hr), hidden_cols(c, yy)]

        def fin():
            for n, d in both:
                recv(inb + n, nbr_rx.at[t, n, mine], dev_y[d])
            total = acc[tile(y)] + nbr_rx[t, 0, mine].astype(F32) + nbr_rx[t, 1, mine].astype(F32)
            if t == 0:
                total, slopes = gelu_pair(total)
                slope[mine] = slopes
            else:
                total = total * slope[mine]
            hb[t, mine, hidden_cols(c, y)] = total.astype(BF)
            p = piece(c, y)
            send(iy, p, p, dev_y[1])
            send(iy + 1, p, p, dev_y[-1])
            send(ih, p, p, dev_c)

        def fwd():
            for n, d in both:
                p, q = piece(c, wrap(y - d)), half(wrap(y - d), n)
                recv(iy + n, p, dev_y[d])
                send(iw + n, q, q, dev_y[d])
                send(ih + 1 + n, p, p, dev_c)

        def opp():
            for n, d in both:
                recv(iw + n, half(wrap(y + 2), n), dev_y[d])
            p = piece(c, wrap(y + 2))
            send(ih + 3, p, p, dev_c)

        def near_in():
            for n, yy in enumerate((y, wrap(y - 1), wrap(y + 1))):
                recv(ih + n, piece(oc, yy), dev_c)

        def far_in():
            recv(ih + 3, piece(oc, wrap(y + 2)), dev_c)

        incoming.setdefault((t, r0 // 256), []).append((near_in, far_in))
        for f in (cmp, ma, mb, mc, md, nb, fin, fwd, opp):
            tasks[f"{f.__name__}_{t}{k}"] = f

    def add_contract(t, half):
        mine = pl.ds(256 * half, 256)
        arrivals = incoming[t, half]

        def whole():
            for near_in, far_in in arrivals:
                near_in()
                far_in()

            def step(n, carry):
                cols = pl.ds(pl.multiple_of(n * 512, 512), 512)
                left = hb[t, mine, :]
                got = dot(left, wo[:, cols]) if t == 0 else dot(left, wi[cols, :], NT)
                part[t, mine, cols] = got.astype(BF)
                return carry

            lax.fori_loop(0, 2, step, 0)

        def product(core, yy):
            units = hidden_cols(core, yy)
            left = hb[t, mine, units]
            return dot(left, wo[units, :]) if t == 0 else dot(left, wi[:, units], NT)

        def ct1():
            for near_in, far_in in arrivals[:-1]:
                near_in()
                far_in()
            arrivals[-1][0]()
            sub[...] = product(c, y)

            def step(n, carry):
                core = lax.rem(c + lax.div(n + 2, 4), 2)
                away = lax.div(n + 2, 4) * (n + 1) + (1 - lax.div(n + 2, 4)) * (2 * n + 3)
                sub[...] += product(core, wrap(y + away))
                return carry

            lax.fori_loop(0, 5, step, 0)

        def ct2():
            arrivals[-1][1]()
            got = sub[...] + product(c, wrap(y + 2)) + product(oc, wrap(y + 2))
            part[t, mine, :] = got.astype(BF)

        if (t, half) == (1, 1):
            tasks["ct1_11"], tasks["ct2_11"] = ct1, ct2
        else:
            tasks[f"ct_{t}{half}"] = whole

    def add_home(t):
        tag = ("m", "d1")[t]
        base = [fresh(19), fresh(19)]

        def group(h, fi):
            picks = ct[fi] if h == 0 else ct[:, fi]
            got = dot(picks.reshape(256, 512), part[t, :, 512 * h:512 * h + 512])
            return got.reshape(4, 64, 512)

        def e0():
            for h in range(2):
                f, s, fd, sd = axes(h)
                spread[t, h, 0] = group(h, wrap(f + 2)).astype(BF)
                for q, far in enumerate((2, 1, -1, 0)):
                    to = wrap(s + far)
                    for n, d in both:
                        send(
                            base[h] + 2 * q + n, spread.at[t, h, 0, to, pl.ds(32 * n, 32)],
                            f_opp.at[t, h, q, n], fd[d],
                        )

        def e1():
            for h in range(2):
                f, s, fd, sd = axes(h)
                for n, d in both:
                    spread[t, h, 1 + n] = group(h, wrap(f + d)).astype(BF)

        def e2():
            for h in range(2):
                home[t, h] = group(h, axes(h)[0])

        def fn(q, far):
            def run():
                for h in range(2):
                    f, s, fd, sd = axes(h)
                    to = wrap(s + far)
                    for n, d in both:
                        recv(base[h] + 2 * q + n, f_opp.at[t, h, q, n], fd[d])
                        here = slice(32 * n, 32 * n + 32)
                        spread[t, h, 1 + n, to, here] = (
                            spread[t, h, 1 + n, to, here].astype(F32)
                            + f_opp[t, h, q, n].astype(F32)
                        ).astype(BF)
                        send(
                            base[h] + 8 + 2 * q + n, spread.at[t, h, 1 + n, to],
                            f_nbr.at[t, h, q, n], fd[d],
                        )
            return run

        def fs(q, far):
            def run():
                for h in range(2):
                    f, s, fd, sd = axes(h)
                    to = wrap(s + far)
                    for n, d in both:
                        recv(base[h] + 8 + 2 * q + n, f_nbr.at[t, h, q, n], fd[d])
                    got = (
                        home[t, h, to]
                        + f_nbr[t, h, q, 0].astype(F32)
                        + f_nbr[t, h, q, 1].astype(F32)
                    )
                    if q == 3:
                        home[t, h, to] = got
                    else:
                        grouped[t, h, q] = got.astype(BF)
                        send(
                            base[h] + 16 + q, grouped.at[t, h, q], s_rx.at[t, h, q], sd[far]
                        )
            return run

        def g3():
            for h in range(2):
                f, s, fd, sd = axes(h)
                got = home[t, h, s]
                for q, far in enumerate((2, 1, -1)):
                    recv(base[h] + 16 + q, s_rx.at[t, h, q], sd[far])
                    got = got + s_rx[t, h, q].astype(F32)
                if t == 0:
                    got = gate[:, 0:1] * got
                slots_out[t, :, 512 * h:512 * h + 512] = got.astype(BF)

        for f in (e0, e1, e2, g3):
            tasks[f"{f.__name__}_{tag}"] = f
        for q, far in enumerate((2, 1, -1, 0)):
            tasks[f"fn{q}_{tag}"] = fn(q, far)
            tasks[f"fs{q}_{tag}"] = fs(q, far)

    moved = {}

    def dwo_tile(j):
        def run():
            here = pl.ds(256 * j, 256)
            got = dot(hb[0, :, here], rows[1], TN).astype(BF)
            if j >= 2:
                moved["o", j - 2].wait()
            dwo[j % 2] = got
            moved["o", j] = local_copy(dwo.at[j % 2], dwo_out.at[here])
        return run

    def dwi_tile(j):
        def run():
            here = pl.ds(256 * j, 256)
            got = dot(rows[0, :, here], hb[1], TN).astype(BF)
            if j >= 2:
                moved["i", j - 2].wait()
            dwi[j % 2] = got
            moved["i", j] = local_copy(dwi.at[j % 2], dwi_out.at[here])
        return run

    for j in range(8):
        tasks[f"dwo{j}"] = dwo_tile(j)
    for j in range(4):
        tasks[f"dwi{j}"] = dwi_tile(j)
    for t in range(2):
        for ph, (b0, nb) in enumerate(PHASES[t]):
            add_gather(t, ph, b0, nb)
        for k, (r0, nr) in enumerate(CHUNKS[t]):
            add_chunk(t, k, r0, nr)
        for half in range(2):
            add_contract(t, half)
        add_home(t)

    entered = False
    for name in ORDER:
        if name == "ag1_00":
            pl.semaphore_wait(barrier, len(partners))
            entered = True
        assert entered or name.startswith("pick")
        tasks.pop(name)()
    assert not tasks

    for d in sent:
        d.wait_send()
    for j in (6, 7):
        moved["o", j].wait()
    for j in (2, 3):
        moved["i", j].wait()


def exchange(chosen, gates, counts, tokens, cotangent, w_in, w_out):
    vmem = pl.BlockSpec(memory_space=pltpu.VMEM)
    anywhere = pl.BlockSpec(memory_space=pl.ANY)
    hbm = pl.BlockSpec(memory_space=pltpu.HBM)

    def v(*shape, dtype=BF):
        return pltpu.VMEM(shape, dtype)

    return pl.pallas_call(
        kernel,
        out_shape=(
            pltpu.VMEM((64, 256), BF),
            pltpu.VMEM((2, 64, 1024), BF),
            pltpu.VMEM((1024, 2048), BF),
            pltpu.VMEM((2048, 1024), BF),
        ),
        in_specs=[vmem] * 3 + [hbm] * 4,
        out_specs=(vmem, vmem, anywhere, anywhere),
        scratch_shapes=[
            v(256, 1024), v(256, 1024), v(1024, 2048), v(2048, 1024),
            v(64, 128, dtype=F32),
            v(2, 2, 4, 4, 4, 16, 512),
            v(4, 4, 8, 128, dtype=jnp.int32),
            v(256, 512), v(256, 768),
            v(4, 4, 64, 512),
            v(2, 512, 1024),
            v(2, 2, 2, 512, 256), v(2, 2, 2, 512, 256),
            v(2, 3, 512, 256),
            v(2, 2, 256, 256),
            v(2, 2, 512, 256),
            v(2, 2, 2, 512, 256, dtype=F32),
            v(512, 256, dtype=F32),
            v(2, 512, 2048),
            v(256, 1024, dtype=F32),
            v(2, 512, 1024),
            v(2, 2, 3, 4, 64, 512),
            v(2, 2, 4, 64, 512, dtype=F32),
            v(2, 2, 4, 2, 32, 512),
            v(2, 2, 4, 2, 64, 512),
            v(2, 2, 3, 64, 512),
            v(2, 2, 3, 64, 512),
            v(2, 256, 2048), v(2, 256, 1024),
            pltpu.SemaphoreType.DMA((N_COPIES,)),
            pltpu.SemaphoreType.DMA((N_COPIES,)),
            pltpu.SemaphoreType.DMA((N_LOCAL,)),
        ],
        compiler_params=pltpu.CompilerParams(
            collective_id=0, has_side_effects=True, vmem_limit_bytes=54 * 2**20
        ),
        cost_estimate=pl.CostEstimate(
            flops=14 * 10**9, bytes_accessed=20 * 2**20, transcendentals=2**19
        ),
    )(chosen, gates, counts, tokens, cotangent, w_in, w_out)


def finish_kernel(
    pick_ref, slots_ref, dwi_in, dwo_in, mixed_ref, d_tok_ref, dwi_out, dwo_out, sem
):
    moves = []
    for src, dst, n in ((dwi_in, dwi_out, 256), (dwo_in, dwo_out, 512)):
        for j in range(4):
            here = pl.ds(n * j, n)
            d = pltpu.make_async_copy(src.at[here], dst.at[here], sem.at[len(moves)])
            d.start()
            moves.append(d)
    mixed_ref[...] = dot(pick_ref[...], slots_ref[0], TN).astype(BF)
    d_tok_ref[...] = dot(pick_ref[...], slots_ref[1], TN).astype(BF)
    for d in moves:
        d.wait()


def finish(pick, slots, d_w_in, d_w_out):
    vmem = pl.BlockSpec(memory_space=pltpu.VMEM)
    anywhere = pl.BlockSpec(memory_space=pl.ANY)
    hbm = pl.BlockSpec(memory_space=pltpu.HBM)
    return pl.pallas_call(
        finish_kernel,
        out_shape=(
            jax.ShapeDtypeStruct((256, 1024), BF),
            jax.ShapeDtypeStruct((256, 1024), BF),
            jax.ShapeDtypeStruct((1024, 2048), BF),
            jax.ShapeDtypeStruct((2048, 1024), BF),
        ),
        in_specs=[vmem, vmem, anywhere, anywhere],
        out_specs=(vmem, vmem, hbm, hbm),
        scratch_shapes=[pltpu.SemaphoreType.DMA((8,))],
        compiler_params=pltpu.CompilerParams(vmem_limit_bytes=8 * 2**20),
        cost_estimate=pl.CostEstimate(
            flops=6 * 10**7, bytes_accessed=18 * 2**20, transcendentals=0
        ),
    )(pick, slots, d_w_in, d_w_out)


def local(tokens, w_in, w_out, chosen, counts, gates, cotangent):
    return finish(*exchange(chosen, gates, counts.reshape(1, 1), tokens, cotangent, w_in, w_out))


def solution(mesh):
    in_specs = (
        P("dp", "expert"),
        P("expert", "dp"),
        P("dp", "expert"),
        P("dp", None),
        P("dp"),
        P("dp", None),
        P("dp", "expert"),
    )
    out_specs = (P("dp", "expert"), P("dp", "expert"), P("expert", "dp"), P("dp", "expert"))
    return jax.shard_map(local, mesh=mesh, in_specs=in_specs, out_specs=out_specs, check_vma=False)
```

```python
import jax
import jax.numpy as jnp
from jax import lax
from jax.experimental import pallas as pl
from jax.experimental.pallas import tpu as pltpu
from jax.sharding import PartitionSpec as P

half_root = 0.7071067811865476
inv_root_tau = 0.3989422804014327

MESH = pl.DeviceIdType.MESH
BF = jnp.bfloat16
F32 = jnp.float32

N_COPIES = 345
N_LOCAL = 24

CHUNKS = ([(0, 128), (128, 128), (256, 128), (384, 128)], [(0, 256), (256, 256)])
PHASES = ([(0, 1), (1, 1), (2, 1), (3, 1)], [(0, 2), (2, 2)])
HOMES = (('m', 0, 0, 512, 0, 64), ('d1', 1, 0, 512, 0, 64))
HOME_SLOTS = 128

ORDER = (
    "pick0", "pick1", "ag1_00", "meta1", "ag1_01", "ag1_02", "ag1_03", "meta2", "ag2_01",
    "ag2_00", "ag3_01", "meta", "ag2_02", "ag1_10", "ag2_03", "ag1_11", "buildc1", "buildc0",
    "ag3_00", "ag4_00", "cmp_00", "ag4_01", "cmp_01", "ma_01", "ma_00", "mb_01", "mb_00",
    "ag3_02", "mc_01", "mc_00", "ag3_03", "ag2_10", "md_01", "nb_01", "md_00", "nb_00", "ag4_02",
    "cmp_02", "ma_02", "ag2_11", "ag4_03", "cmp_03", "mb_02", "ma_03", "fin_01", "mc_02", "mb_03",
    "fin_00", "ag3_10", "mc_03", "md_02", "nb_02", "ag3_11", "md_03", "nb_03", "buildct",
    "fwd_00", "fwd_01", "ag4_10", "cmp_10", "ma_10", "fin_02", "ag4_11", "cmp_11", "fin_03",
    "ma_11", "mb_10", "mb_11", "mc_10", "fwd_02", "mc_11", "opp_01", "fwd_03", "opp_00", "md_10",
    "md_11", "nb_10", "ct_00", "opp_02", "nb_11", "opp_03", "ct_01", "fin_10", "e0_m", "fin_11",
    "e1_m", "fn0_m", "fwd_10", "fn1_m", "fn2_m", "fn3_m", "dwo0", "dwo1", "e2_m", "fwd_11",
    "dwo2", "fs0_m", "fs1_m", "opp_10", "ct1_11", "fs2_m", "opp_11", "ct_10", "ct2_11", "e0_d1",
    "e1_d1", "dwo3", "fn0_d1", "fn1_d1", "dwo4", "fn2_d1", "dwi0", "fn3_d1", "dwo5", "dwo6",
    "dwi1", "e2_d1", "dwo7", "fs0_d1", "dwi2", "fs1_d1", "fs2_d1", "fs3_d1", "fs3_m", "g3_m",
    "dwi3", "g3_d1",
)

NN = (((1,), (0,)), ((), ()))
NT = (((1,), (1,)), ((), ()))
TN = (((0,), (0,)), ((), ()))


def dot(a, b, dims=NN):
    return lax.dot_general(a, b, dims, preferred_element_type=F32)


def gelu_pair(pre_act):
    cdf_part = 0.5 * (1.0 + lax.erf(pre_act * half_root))
    slopes = cdf_part + pre_act * jnp.exp(-0.5 * pre_act * pre_act) * inv_root_tau
    return (pre_act * cdf_part, slopes)


def wrap(v):
    return lax.rem(v + 8, 4)


def kernel(
    chosen_ref, gates_ref, count_ref, tok_hbm, cot_hbm, wi_hbm, wo_hbm,
    pick_out, slots_out, dwi_out, dwo_out,
    tok, cot, wi, wo, gate, ag, cnt, c_low, c_high, ct, rows, xs, xr, ps, opp_rx, nbr_rx, acc, slope, hb,
    sub, part, spread, home, f_opp, f_nbr, grouped, s_rx, early, dwi, dwo,
    send_sem, recv_sem, local_sem,
):
    dp, ex = lax.axis_index("dp"), lax.axis_index("expert")
    x, z = lax.div(dp, 4), lax.rem(dp, 4)
    y, c = lax.div(ex, 2), lax.rem(ex, 2)
    oc = 1 - c
    dev_x = {d: (wrap(x + d) * 4 + z, ex) for d in (1, -1, 2)}
    dev_z = {d: (x * 4 + wrap(z + d), ex) for d in (1, -1, 2)}
    dev_y = {d: (dp, wrap(y + d) * 2 + c) for d in (1, -1)}
    dev_c = (dp, y * 2 + oc)
    both = ((0, 1), (1, -1))
    three = ((0, 1), (1, -1), (2, 2))

    counter = [0]
    sent = []

    def fresh(n):
        first = counter[0]
        counter[0] += n
        assert counter[0] <= N_COPIES
        return first

    def copy(i, src, dst, dev):
        return pltpu.make_async_remote_copy(
            src_ref=src, dst_ref=dst, send_sem=send_sem.at[i], recv_sem=recv_sem.at[i],
            device_id=dev, device_id_type=MESH,
        )

    def send(i, src, dst, dev):
        d = copy(i, src, dst, dev)
        d.start()
        sent.append(d)

    def recv(i, landing, dev):
        copy(i, landing, landing, dev).wait_recv()

    opened = []

    def local_copy(src, dst):
        d = pltpu.make_async_copy(src, dst, local_sem.at[len(opened)])
        d.start()
        opened.append(d)
        return d

    load = {
        "tok": local_copy(tok_hbm, tok),
        "cot": local_copy(cot_hbm, cot),
        0: local_copy(wi_hbm, wi),
        1: local_copy(wo_hbm, wo),
    }

    barrier = pltpu.get_barrier_semaphore()
    partners = [dev_x[d] for d in dev_x] + [dev_z[d] for d in dev_z] + [dev_y[1], dev_y[-1], dev_c]
    for dev in partners:
        pl.semaphore_signal(barrier, inc=1, device_id=dev, device_id_type=MESH)

    tasks = {}

    def column(row):
        here = lax.broadcasted_iota(jnp.int32, (64, 64), 0)
        there = lax.broadcasted_iota(jnp.int32, (64, 64), 1)
        wide = jnp.broadcast_to(row.astype(F32), (64, 64))
        return jnp.sum(jnp.where(here == there, wide, 0.0), axis=1, keepdims=True)

    def pick0():
        place = jnp.broadcast_to(column(chosen_ref[...]), (64, 256)).astype(jnp.int32)
        spot = lax.broadcasted_iota(jnp.int32, (64, 256), 1)
        slot = lax.broadcasted_iota(jnp.int32, (64, 256), 0)
        held = jnp.broadcast_to(count_ref[...], (64, 256))
        hit = jnp.where(place == spot, 1.0, 0.0) * jnp.where(slot < held, 1.0, 0.0)
        pick_out[...] = hit.astype(BF)
        gate[...] = jnp.broadcast_to(column(gates_ref[...]), (64, 128))
        cnt[x, z] = jnp.broadcast_to(count_ref[...], (8, 128))
        load["tok"].wait()
        keep(0, dot(pick_out[...], tok[...]).astype(BF))

    def pick1():
        load["cot"].wait()
        keep(1, (gate[:, 0:1] * dot(pick_out[...], cot[...])).astype(BF))

    def keep(t, got):
        for b in range(4):
            for h in range(2):
                ag[t, h, b, x, z] = got[16 * b:16 * b + 16, 512 * h:512 * h + 512]

    tasks["pick0"], tasks["pick1"] = pick0, pick1

    def axes(h):
        return (x, z, dev_x, dev_z) if h == 0 else (z, x, dev_z, dev_x)

    def add_gather(t, ph, b0, nb):
        base = [fresh(8), fresh(8)]
        blocks = pl.ds(b0, nb)
        direct = (t, ph) == (0, 0)

        def blk(h, fi, si):
            return ag.at[(t, h, blocks) + ((fi, si) if h == 0 else (si, fi))]

        def grp(h, si, first, n):
            many = pl.ds(first, n)
            return ag.at[(t, h, blocks) + ((many, si) if h == 0 else (si, many))]

        def ag1():
            for h in range(2):
                f, s, fd, sd = axes(h)
                for n, d in three:
                    send(base[h] + n, blk(h, f, s), blk(h, f, s), fd[d])

        def ag2():
            for h in range(2):
                f, s, fd, sd = axes(h)
                for n, d in three:
                    recv(base[h] + n, blk(h, wrap(f - d), s), fd[d])
                for n, d in three if direct else both:
                    send(base[h] + 3 + n, grp(h, s, 0, 4), grp(h, s, 0, 4), sd[d])

        def ag3():
            for h in range(2):
                f, s, fd, sd = axes(h)
                for n, d in three if direct else both:
                    recv(base[h] + 3 + n, grp(h, wrap(s - d), 0, 4), sd[d])
                    if not direct:
                        g = grp(h, wrap(s - d), 2 * n, 2)
                        send(base[h] + 6 + n, g, g, sd[d])

        def ag4():
            for h in range(2):
                f, s, fd, sd = axes(h)
                for n, d in both:
                    if not direct:
                        recv(base[h] + 6 + n, grp(h, wrap(s + 2), 2 * n, 2), sd[d])

        for name, f in (("ag1", ag1), ("ag2", ag2), ("ag3", ag3), ("ag4", ag4)):
            tasks[f"{name}_{t}{ph}"] = f

    meta_base = fresh(6)

    def meta1():
        for n, d in three:
            send(meta_base + n, cnt.at[x, z], cnt.at[x, z], dev_x[d])

    def meta2():
        for n, d in three:
            recv(meta_base + n, cnt.at[wrap(x - d), z], dev_x[d])
        for n, d in three:
            send(meta_base + 3 + n, cnt.at[:, z], cnt.at[:, z], dev_z[d])

    def meta():
        for n, d in three:
            recv(meta_base + 3 + n, cnt.at[:, wrap(z - d)], dev_z[d])

    tasks.update(meta1=meta1, meta2=meta2, meta=meta)

    def places(upto):
        total = jnp.zeros((8, 128), jnp.int32)
        found = []
        for b in range(upto):
            found.append([])
            for i in range(16):
                held = jnp.clip(cnt[i // 4, i % 4] - 16 * b, 0, 16)
                found[b].append((total, held))
                total = total + held
        return found

    def build_c(out, blocks, first_row):
        found = places(blocks[-1] + 1)
        lane = lax.broadcasted_iota(jnp.int32, (8, 128), 1)
        part_of, slot = lane // 16, lane % 16
        row = lax.broadcasted_iota(jnp.int32, (256, 128), 0) + first_row
        for b in blocks:
            for j in range(2):
                start, held = found[b][8 * j]
                for i in range(1, 8):
                    start = jnp.where(part_of == i, found[b][8 * j + i][0], start)
                    held = jnp.where(part_of == i, found[b][8 * j + i][1], held)
                place = jnp.where(slot < held, start + slot, -1)
                hit = jnp.broadcast_to(place[0:1], (256, 128)) == row
                at = 256 * (b - blocks[0]) + 128 * j
                out[:, at:at + 128] = jnp.where(hit, 1.0, 0.0).astype(BF)

    def buildc0():
        build_c(c_low, (0, 1), 0)

    def buildc1():
        build_c(c_high, (1, 2, 3), 256)

    def buildct():
        found = places(4)
        slot = lax.broadcasted_iota(jnp.int32, (16, 128), 0)
        lane = lax.broadcasted_iota(jnp.int32, (16, 128), 1)
        for i in range(16):
            for b in range(4):
                start = jnp.broadcast_to(found[b][i][0][0:1], (16, 128))
                held = jnp.broadcast_to(found[b][i][1][0:1], (16, 128))
                place = jnp.where(slot < held, start + slot, -1)
                for j in range(4):
                    hit = place == lane + 128 * j
                    ct[i // 4, i % 4, 16 * b:16 * b + 16, 128 * j:128 * j + 128] = jnp.where(
                        hit, 1.0, 0.0
                    ).astype(BF)

    tasks.update(buildc0=buildc0, buildc1=buildc1, buildct=buildct)

    def hidden_cols(core, yy, width=256):
        return pl.ds(pl.multiple_of(core * 1024 + yy * width, width), width)

    loaded = set()
    incoming = {}

    def add_chunk(t, k, r0, nr):
        mine = pl.ds(r0, nr)
        hr = nr // 2
        ic, io, inb = fresh(2), fresh(2), fresh(2)
        iy, iw, ih = fresh(2), fresh(2), fresh(4)
        far = lax.div(wrap(y + 2), 2)
        near = 1 - far

        def cmp():
            b0, b1 = (0 if r0 < 256 else 1), (r0 + nr) // 128
            width = 256 * (b1 - b0)
            at = r0 % 256
            picks = (c_low if r0 < 256 else c_high)[at:at + nr, :width]
            for h in range(2):
                got = dot(picks, ag[t, h, b0:b1].reshape(width, 512))
                rows[t, mine, 512 * h:512 * h + 512] = got.astype(BF)

        def pair(core, p):
            left = rows[t, mine, :]
            if t == 0:
                return dot(left, wi[:, hidden_cols(core, p, 512)])
            return dot(left, wo[hidden_cols(core, p, 512), :], NT)

        def for_other(p, n):
            got = pair(oc, p).astype(BF)
            xs[t, p, 0, mine] = got[:, :256]
            xs[t, p, 1, mine] = got[:, 256:]
            tiles = pl.ds(0, 2)
            send(ic + n, xs.at[t, p, tiles, mine], xr.at[t, p, tiles, mine], dev_c)

        def for_self(p, n):
            got = pair(c, p)
            recv(ic + n, xr.at[t, p, pl.ds(0, 2), mine], dev_c)
            acc[t, p, 0, mine] = got[:, :256] + xr[t, p, 0, mine].astype(F32)
            acc[t, p, 1, mine] = got[:, 256:] + xr[t, p, 1, mine].astype(F32)

        def tile(yy):
            return (t, lax.div(yy, 2), lax.rem(yy, 2), mine)

        def ma():
            if t not in loaded:
                loaded.add(t)
                load[t].wait()
            for_other(far, 0)

        def opp_landing(n):
            return (t, n, pl.ds(r0 // 2, hr))

        def mb():
            for_self(far, 0)
            ps[t, 0, mine] = acc[tile(wrap(y + 2))].astype(BF)
            for n, d in both:
                send(
                    io + n, ps.at[t, 0, pl.ds(r0 + hr * n, hr)], opp_rx.at[opp_landing(n)],
                    dev_y[d],
                )

        def mc():
            for_other(near, 1)

        def md():
            for_self(near, 1)

        def nb():
            for n, d in both:
                recv(io + n, opp_rx.at[opp_landing(n)], dev_y[d])
                got = acc[tile(wrap(y + d))]
                here = slice(hr * n, hr * n + hr)
                away = slice(hr - hr * n, nr - hr * n)
                added = got[here] + opp_rx[opp_landing(n)].astype(F32)
                ps[t, 1 + n, pl.ds(r0 + here.start, hr)] = added.astype(BF)
                ps[t, 1 + n, pl.ds(r0 + away.start, hr)] = got[away].astype(BF)
                send(inb + n, ps.at[t, 1 + n, mine], nbr_rx.at[t, n, mine], dev_y[d])

        def piece(core, yy):
            return hb.at[t, mine, hidden_cols(core, yy)]

        def half(yy, n):
            return hb.at[t, pl.ds(r0 + hr * n, hr), hidden_cols(c, yy)]

        def fin():
            for n, d in both:
                recv(inb + n, nbr_rx.at[t, n, mine], dev_y[d])
            total = acc[tile(y)] + nbr_rx[t, 0, mine].astype(F32) + nbr_rx[t, 1, mine].astype(F32)
            if t == 0:
                total, slopes = gelu_pair(total)
                slope[mine] = slopes
            else:
                total = total * slope[mine]
            hb[t, mine, hidden_cols(c, y)] = total.astype(BF)
            p = piece(c, y)
            send(iy, p, p, dev_y[1])
            send(iy + 1, p, p, dev_y[-1])
            send(ih, p, p, dev_c)

        def fwd():
            for n, d in both:
                p, q = piece(c, wrap(y - d)), half(wrap(y - d), n)
                recv(iy + n, p, dev_y[d])
                send(iw + n, q, q, dev_y[d])
                send(ih + 1 + n, p, p, dev_c)

        def opp():
            for n, d in both:
                recv(iw + n, half(wrap(y + 2), n), dev_y[d])
            p = piece(c, wrap(y + 2))
            send(ih + 3, p, p, dev_c)

        def near_in():
            for n, yy in enumerate((y, wrap(y - 1), wrap(y + 1))):
                recv(ih + n, piece(oc, yy), dev_c)

        def far_in():
            recv(ih + 3, piece(oc, wrap(y + 2)), dev_c)

        incoming.setdefault((t, r0 // 256), []).append((near_in, far_in))
        for f in (cmp, ma, mb, mc, md, nb, fin, fwd, opp):
            tasks[f"{f.__name__}_{t}{k}"] = f

    def add_contract(t, half):
        mine = pl.ds(256 * half, 256)
        arrivals = incoming[t, half]

        def whole():
            for near_in, far_in in arrivals:
                near_in()
                far_in()

            def step(n, carry):
                cols = pl.ds(pl.multiple_of(n * 512, 512), 512)
                left = hb[t, mine, :]
                got = dot(left, wo[:, cols]) if t == 0 else dot(left, wi[cols, :], NT)
                part[t, mine, cols] = got.astype(BF)
                return carry

            lax.fori_loop(0, 2, step, 0)

        def product(core, yy):
            units = hidden_cols(core, yy)
            left = hb[t, mine, units]
            return dot(left, wo[units, :]) if t == 0 else dot(left, wi[:, units], NT)

        def ct1():
            for near_in, far_in in arrivals[:-1]:
                near_in()
                far_in()
            arrivals[-1][0]()
            sub[...] = product(c, y)

            def step(n, carry):
                core = lax.rem(c + lax.div(n + 2, 4), 2)
                away = lax.div(n + 2, 4) * (n + 1) + (1 - lax.div(n + 2, 4)) * (2 * n + 3)
                sub[...] += product(core, wrap(y + away))
                return carry

            lax.fori_loop(0, 5, step, 0)

        def ct2():
            sub[...] += product(c, wrap(y + 2))
            arrivals[-1][1]()
            part[t, mine, :] = (sub[...] + product(oc, wrap(y + 2))).astype(BF)

        if (t, half) == (1, 1):
            tasks["ct1_11"], tasks["ct2_11"] = ct1, ct2
        else:
            tasks[f"ct_{t}{half}"] = whole

    def add_home(tag, t, r0, nr, s0, ns, at, in_four):
        base = [fresh(19), fresh(19)]
        mine = pl.ds(at, ns)
        order = (2, 1, -1, 0)

        def targets(q, s):
            return pl.ds(wrap(s + order[q]), 1) if in_four else pl.ds(0, 4)

        def group(h, fi):
            slots, those = slice(s0, s0 + ns), slice(r0, r0 + nr)
            picks = ct[fi, :, slots, those] if h == 0 else ct[:, fi, slots, those]
            cols = slice(512 * h, 512 * h + 512)
            return dot(picks.reshape(4 * ns, nr), part[t, those, cols]).reshape(4, ns, 512)

        def e0():
            for h in range(2):
                f, s, fd, sd = axes(h)
                spread[h, 0, :, mine] = group(h, wrap(f + 2)).astype(BF)
                for q in range(4 if in_four else 1):
                    to = targets(q, s)
                    for n, d in both:
                        send(
                            base[h] + 2 * q + n, spread.at[h, 0, to, mine, pl.ds(256 * n, 256)],
                            f_opp.at[h, n, to, mine], fd[d],
                        )

        def e1():
            for h in range(2):
                f, s, fd, sd = axes(h)
                for n, d in both:
                    spread[h, 1 + n, :, mine] = group(h, wrap(f + d)).astype(BF)

        def e2():
            for h in range(2):
                home[h, :, mine] = group(h, axes(h)[0])

        def fn(q):
            def run():
                for h in range(2):
                    f, s, fd, sd = axes(h)
                    to = targets(q, s)
                    for n, d in both:
                        recv(base[h] + 2 * q + n, f_opp.at[h, n, to, mine], fd[d])
                        cols = slice(256 * n, 256 * n + 256)
                        spread[h, 1 + n, to, mine, cols] = (
                            spread[h, 1 + n, to, mine, cols].astype(F32)
                            + f_opp[h, n, to, mine].astype(F32)
                        ).astype(BF)
                        send(
                            base[h] + 8 + 2 * q + n, spread.at[h, 1 + n, to, mine],
                            f_nbr.at[h, n, to, mine], fd[d],
                        )
            return run

        def fs(q):
            def run():
                for h in range(2):
                    f, s, fd, sd = axes(h)
                    to = targets(q, s)
                    for n, d in both:
                        recv(base[h] + 8 + 2 * q + n, f_nbr.at[h, n, to, mine], fd[d])
                    got = (
                        home[h, to, mine]
                        + f_nbr[h, 0, to, mine].astype(F32)
                        + f_nbr[h, 1, to, mine].astype(F32)
                    )
                    home[h, to, mine] = got
                    grouped[h, to, mine] = got.astype(BF)
                    for p in (q,) if in_four else range(4):
                        if p < 3:
                            away = wrap(s + order[p])
                            send(
                                base[h] + 16 + p, grouped.at[h, away, mine],
                                s_rx.at[h, p, mine], sd[order[p]],
                            )
            return run

        def g3():
            for h in range(2):
                f, s, fd, sd = axes(h)
                got = home[h, s, mine]
                for p in range(3):
                    recv(base[h] + 16 + p, s_rx.at[h, p, mine], sd[order[p]])
                    got = got + s_rx[h, p, mine].astype(F32)
                cols = slice(512 * h, 512 * h + 512)
                if ns == 32:
                    early[t, :, cols] = got
                    continue
                pieces = ((slice(0, 64), got),)
                if ns == 48:
                    pieces = (
                        (slice(0, 16), early[t, 0:16, cols]),
                        (slice(16, 32), early[t, 16:32, cols] + got[0:16]),
                        (slice(32, 64), got[16:48]),
                    )
                for slots, value in pieces:
                    if t == 0:
                        value = gate[slots, 0:1] * value
                    slots_out[t, slots, cols] = value.astype(BF)

        for f in (e0, e1, e2, g3):
            tasks[f"{f.__name__}_{tag}"] = f
        for q in range(4 if in_four else 1):
            tasks[f"fn{q}_{tag}"] = fn(q)
            tasks[f"fs{q}_{tag}"] = fs(q)

    moved = {}

    def dwo_tile(j):
        def run():
            here = pl.ds(256 * j, 256)
            got = dot(hb[0, :, here], rows[1], TN).astype(BF)
            if j >= 2:
                moved["o", j - 2].wait()
            dwo[j % 2] = got
            moved["o", j] = local_copy(dwo.at[j % 2], dwo_out.at[here])
        return run

    def dwi_tile(j):
        def run():
            here = pl.ds(256 * j, 256)
            got = dot(rows[0, :, here], hb[1], TN).astype(BF)
            if j >= 2:
                moved["i", j - 2].wait()
            dwi[j % 2] = got
            moved["i", j] = local_copy(dwi.at[j % 2], dwi_out.at[here])
        return run

    for j in range(8):
        tasks[f"dwo{j}"] = dwo_tile(j)
    for j in range(4):
        tasks[f"dwi{j}"] = dwi_tile(j)
    at = 0
    for tag, t, r0, nr, s0, ns in HOMES:
        add_home(tag, t, r0, nr, s0, ns, at, ns == 64 or tag == "d1")
        at += ns
    for t in range(2):
        for ph, (b0, nb) in enumerate(PHASES[t]):
            add_gather(t, ph, b0, nb)
        for k, (r0, nr) in enumerate(CHUNKS[t]):
            add_chunk(t, k, r0, nr)
        for half in range(2):
            add_contract(t, half)

    entered = False
    for name in ORDER:
        if name == "ag1_00":
            pl.semaphore_wait(barrier, len(partners))
            entered = True
        assert entered or name.startswith("pick")
        tasks.pop(name)()
    assert not tasks

    for d in sent:
        d.wait_send()
    for j in (6, 7):
        moved["o", j].wait()
    for j in (2, 3):
        moved["i", j].wait()


def exchange(chosen, gates, counts, tokens, cotangent, w_in, w_out):
    vmem = pl.BlockSpec(memory_space=pltpu.VMEM)
    anywhere = pl.BlockSpec(memory_space=pl.ANY)
    hbm = pl.BlockSpec(memory_space=pltpu.HBM)

    def v(*shape, dtype=BF):
        return pltpu.VMEM(shape, dtype)

    return pl.pallas_call(
        kernel,
        out_shape=(
            pltpu.VMEM((64, 256), BF),
            pltpu.VMEM((2, 64, 1024), BF),
            pltpu.VMEM((1024, 2048), BF),
            pltpu.VMEM((2048, 1024), BF),
        ),
        in_specs=[vmem] * 3 + [hbm] * 4,
        out_specs=(vmem, vmem, anywhere, anywhere),
        scratch_shapes=[
            v(256, 1024), v(256, 1024), v(1024, 2048), v(2048, 1024),
            v(64, 128, dtype=F32),
            v(2, 2, 4, 4, 4, 16, 512),
            v(4, 4, 8, 128, dtype=jnp.int32),
            v(256, 512), v(256, 768),
            v(4, 4, 64, 512),
            v(2, 512, 1024),
            v(2, 2, 2, 512, 256), v(2, 2, 2, 512, 256),
            v(2, 3, 512, 256),
            v(2, 2, 256, 256),
            v(2, 2, 512, 256),
            v(2, 2, 2, 512, 256, dtype=F32),
            v(512, 256, dtype=F32),
            v(2, 512, 2048),
            v(256, 1024, dtype=F32),
            v(2, 512, 1024),
            v(2, 3, 4, HOME_SLOTS, 512),
            v(2, 4, HOME_SLOTS, 512, dtype=F32),
            v(2, 2, 4, HOME_SLOTS, 256),
            v(2, 2, 4, HOME_SLOTS, 512),
            v(2, 4, HOME_SLOTS, 512),
            v(2, 3, HOME_SLOTS, 512),
            v(2, 32, 1024, dtype=F32),
            v(2, 256, 2048), v(2, 256, 1024),
            pltpu.SemaphoreType.DMA((N_COPIES,)),
            pltpu.SemaphoreType.DMA((N_COPIES,)),
            pltpu.SemaphoreType.DMA((N_LOCAL,)),
        ],
        compiler_params=pltpu.CompilerParams(
            collective_id=0, has_side_effects=True, vmem_limit_bytes=54 * 2**20
        ),
        cost_estimate=pl.CostEstimate(
            flops=14 * 10**9, bytes_accessed=20 * 2**20, transcendentals=2**19
        ),
    )(chosen, gates, counts, tokens, cotangent, w_in, w_out)


def finish_kernel(
    pick_ref, slots_ref, dwi_in, dwo_in, mixed_out, d_tok_out, dwi_out, dwo_out, spot, sem
):
    moves = []
    for src, dst, n in ((dwi_in, dwi_out, 256), (dwo_in, dwo_out, 512)):
        for j in range(4):
            here = pl.ds(n * j, n)
            d = pltpu.make_async_copy(src.at[here], dst.at[here], sem.at[len(moves)])
            d.start()
            moves.append(d)
    for t, out in enumerate((mixed_out, d_tok_out)):
        spot[t] = dot(pick_ref[...], slots_ref[t], TN).astype(BF)
        d = pltpu.make_async_copy(spot.at[t], out, sem.at[len(moves)])
        d.start()
        moves.append(d)
    for d in moves:
        d.wait()


def finish(pick, slots, d_w_in, d_w_out):
    vmem = pl.BlockSpec(memory_space=pltpu.VMEM)
    anywhere = pl.BlockSpec(memory_space=pl.ANY)
    hbm = pl.BlockSpec(memory_space=pltpu.HBM)
    return pl.pallas_call(
        finish_kernel,
        out_shape=(
            jax.ShapeDtypeStruct((256, 1024), BF),
            jax.ShapeDtypeStruct((256, 1024), BF),
            jax.ShapeDtypeStruct((1024, 2048), BF),
            jax.ShapeDtypeStruct((2048, 1024), BF),
        ),
        in_specs=[vmem, vmem, anywhere, anywhere],
        out_specs=(hbm, hbm, hbm, hbm),
        scratch_shapes=[pltpu.VMEM((2, 256, 1024), BF), pltpu.SemaphoreType.DMA((10,))],
        compiler_params=pltpu.CompilerParams(vmem_limit_bytes=8 * 2**20),
        cost_estimate=pl.CostEstimate(
            flops=6 * 10**7, bytes_accessed=18 * 2**20, transcendentals=0
        ),
    )(pick, slots, d_w_in, d_w_out)


def local(tokens, w_in, w_out, chosen, counts, gates, cotangent):
    return finish(*exchange(chosen, gates, counts.reshape(1, 1), tokens, cotangent, w_in, w_out))


def solution(mesh):
    in_specs = (
        P("dp", "expert"),
        P("expert", "dp"),
        P("dp", "expert"),
        P("dp", None),
        P("dp"),
        P("dp", None),
        P("dp", "expert"),
    )
    out_specs = (P("dp", "expert"), P("dp", "expert"), P("expert", "dp"), P("dp", "expert"))
    return jax.shard_map(local, mesh=mesh, in_specs=in_specs, out_specs=out_specs, check_vma=False)
```

```python
import jax
import jax.numpy as jnp
from jax import lax
from jax.experimental import pallas as pl
from jax.experimental.pallas import tpu as pltpu
from jax.sharding import PartitionSpec as P

half_root = 0.7071067811865476
inv_root_tau = 0.3989422804014327

MESH = pl.DeviceIdType.MESH
BF = jnp.bfloat16
F32 = jnp.float32

N_COPIES = 300
N_LOCAL = 24

CHUNKS = ([(0, 128), (128, 128), (256, 128), (384, 128)], [(0, 256), (256, 256)])
PHASES = ([(0, 1), (1, 1), (2, 1), (3, 1)], [(0, 2), (2, 2)])

ORDER = (
    "pick0", "ag1_00", "meta1", "ag1_01", "ag1_02", "ag1_03", "meta2", "ag2_01", "ag2_00", "meta",
    "ag3_01", "buildct", "ag2_02", "ag2_03", "buildc0", "buildc1", "pick1", "ag1_10", "ag3_00",
    "ag4_01", "ag4_00", "cmp_01", "ma_01", "cmp_00", "ma_00", "mb_01", "ag3_02", "mc_01", "mb_00",
    "ag3_03", "mc_00", "md_01", "ag1_11", "md_00", "nb_01", "ag2_10", "ag4_02", "cmp_02", "ma_02",
    "nb_00", "ag4_03", "cmp_03", "ma_03", "mb_02", "mc_02", "mb_03", "ag2_11", "fin_01", "md_02",
    "mc_03", "fin_00", "nb_02", "ag3_10", "md_03", "nb_03", "fwd_00", "ag3_11", "fwd_01",
    "ag4_10", "cmp_10", "fin_02", "ma_10", "fin_03", "mb_10", "ag4_11", "cmp_11", "ma_11",
    "mc_10", "fwd_02", "opp_00", "mb_11", "mc_11", "opp_01", "fwd_03", "md_10", "nb_10", "md_11",
    "opp_02", "ct_00", "opp_03", "nb_11", "ct_01", "fin_10", "e0_m", "dwo0", "e1_m", "fin_11",
    "fn0_m", "fn1_m", "dwo1", "fwd_10", "fn2_m", "e2_m", "dwo2", "dwo3", "fwd_11", "fn3_m",
    "fs0_m", "fs1_m", "opp_10", "ct1_11", "fs2_m", "opp_11", "ct_10", "ct2_11", "e0_d1", "e1_d1",
    "dwo4", "dwi0", "fn0_d1", "fn1_d1", "fn2_d1", "dwo5", "dwi1", "e2_d1", "fn3_d1", "fs0_d1",
    "fs3_m", "dwo6", "fs1_d1", "dwi2", "fs2_d1", "fs3_d1", "dwi3", "g3_m", "dwo7", "g3_d1",
)

NN = (((1,), (0,)), ((), ()))
NT = (((1,), (1,)), ((), ()))
TN = (((0,), (0,)), ((), ()))


def dot(a, b, dims=NN):
    return lax.dot_general(a, b, dims, preferred_element_type=F32)


def gelu_pair(pre_act):
    cdf_part = 0.5 * (1.0 + lax.erf(pre_act * half_root))
    slopes = cdf_part + pre_act * jnp.exp(-0.5 * pre_act * pre_act) * inv_root_tau
    return (pre_act * cdf_part, slopes)


def wrap(v):
    return lax.rem(v + 8, 4)


def kernel(
    chosen_ref, gates_ref, count_ref, tok_hbm, cot_hbm, wi_hbm, wo_hbm,
    pick_out, slots_out, dwi_out, dwo_out,
    tok, cot, wi, wo, gate, ag, cnt, c_low, c_high, ct, rows, xs, xr, ps, opp_rx, nbr_rx, acc, slope, hb,
    sub, part, spread, home, f_opp, f_nbr, grouped, s_rx, dwi, dwo,
    send_sem, recv_sem, local_sem,
):
    dp, ex = lax.axis_index("dp"), lax.axis_index("expert")
    x, z = lax.div(dp, 4), lax.rem(dp, 4)
    y, c = lax.div(ex, 2), lax.rem(ex, 2)
    oc = 1 - c
    dev_x = {d: (wrap(x + d) * 4 + z, ex) for d in (1, -1, 2)}
    dev_z = {d: (x * 4 + wrap(z + d), ex) for d in (1, -1, 2)}
    dev_y = {d: (dp, wrap(y + d) * 2 + c) for d in (1, -1)}
    dev_c = (dp, y * 2 + oc)
    both = ((0, 1), (1, -1))
    three = ((0, 1), (1, -1), (2, 2))

    counter = [0]
    sent = []

    def fresh(n):
        first = counter[0]
        counter[0] += n
        assert counter[0] <= N_COPIES
        return first

    def copy(i, src, dst, dev):
        return pltpu.make_async_remote_copy(
            src_ref=src, dst_ref=dst, send_sem=send_sem.at[i], recv_sem=recv_sem.at[i],
            device_id=dev, device_id_type=MESH,
        )

    def send(i, src, dst, dev):
        d = copy(i, src, dst, dev)
        d.start()
        sent.append(d)

    def recv(i, landing, dev):
        copy(i, landing, landing, dev).wait_recv()

    opened = []

    def local_copy(src, dst):
        d = pltpu.make_async_copy(src, dst, local_sem.at[len(opened)])
        d.start()
        opened.append(d)
        return d

    load = {
        "tok": local_copy(tok_hbm, tok),
        "cot": local_copy(cot_hbm, cot),
        0: local_copy(wi_hbm, wi),
        1: local_copy(wo_hbm, wo),
    }

    barrier = pltpu.get_barrier_semaphore()
    partners = [dev_x[d] for d in dev_x] + [dev_z[d] for d in dev_z] + [dev_y[1], dev_y[-1], dev_c]
    for dev in partners:
        pl.semaphore_signal(barrier, inc=1, device_id=dev, device_id_type=MESH)

    tasks = {}

    def column(row):
        here = lax.broadcasted_iota(jnp.int32, (64, 64), 0)
        there = lax.broadcasted_iota(jnp.int32, (64, 64), 1)
        wide = jnp.broadcast_to(row.astype(F32), (64, 64))
        return jnp.sum(jnp.where(here == there, wide, 0.0), axis=1, keepdims=True)

    def pick0():
        place = jnp.broadcast_to(column(chosen_ref[...]), (64, 256)).astype(jnp.int32)
        spot = lax.broadcasted_iota(jnp.int32, (64, 256), 1)
        slot = lax.broadcasted_iota(jnp.int32, (64, 256), 0)
        held = jnp.broadcast_to(count_ref[...], (64, 256))
        hit = jnp.where(place == spot, 1.0, 0.0) * jnp.where(slot < held, 1.0, 0.0)
        pick_out[...] = hit.astype(BF)
        gate[...] = jnp.broadcast_to(column(gates_ref[...]), (64, 128))
        cnt[x, z] = jnp.broadcast_to(count_ref[...], (8, 128))
        load["tok"].wait()
        keep(0, dot(pick_out[...], tok[...]).astype(BF))

    def pick1():
        load["cot"].wait()
        keep(1, (gate[:, 0:1] * dot(pick_out[...], cot[...])).astype(BF))

    def keep(t, got):
        for b in range(4):
            for h in range(2):
                ag[t, h, b, x, z] = got[16 * b:16 * b + 16, 512 * h:512 * h + 512]

    tasks["pick0"], tasks["pick1"] = pick0, pick1

    def axes(h):
        return (x, z, dev_x, dev_z) if h == 0 else (z, x, dev_z, dev_x)

    def add_gather(t, ph, b0, nb):
        base = [fresh(8), fresh(8)]
        blocks = pl.ds(b0, nb)
        direct = (t, ph) == (0, 0)

        def blk(h, fi, si):
            return ag.at[(t, h, blocks) + ((fi, si) if h == 0 else (si, fi))]

        def grp(h, si, first, n):
            many = pl.ds(first, n)
            return ag.at[(t, h, blocks) + ((many, si) if h == 0 else (si, many))]

        def ag1():
            for h in range(2):
                f, s, fd, sd = axes(h)
                for n, d in three:
                    send(base[h] + n, blk(h, f, s), blk(h, f, s), fd[d])

        def ag2():
            for h in range(2):
                f, s, fd, sd = axes(h)
                for n, d in three:
                    recv(base[h] + n, blk(h, wrap(f - d), s), fd[d])
                for n, d in three if direct else both:
                    send(base[h] + 3 + n, grp(h, s, 0, 4), grp(h, s, 0, 4), sd[d])

        def ag3():
            for h in range(2):
                f, s, fd, sd = axes(h)
                for n, d in three if direct else both:
                    recv(base[h] + 3 + n, grp(h, wrap(s - d), 0, 4), sd[d])
                    if not direct:
                        g = grp(h, wrap(s - d), 2 * n, 2)
                        send(base[h] + 6 + n, g, g, sd[d])

        def ag4():
            for h in range(2):
                f, s, fd, sd = axes(h)
                for n, d in both:
                    if not direct:
                        recv(base[h] + 6 + n, grp(h, wrap(s + 2), 2 * n, 2), sd[d])

        for name, f in (("ag1", ag1), ("ag2", ag2), ("ag3", ag3), ("ag4", ag4)):
            tasks[f"{name}_{t}{ph}"] = f

    meta_base = fresh(6)

    def meta1():
        for n, d in three:
            send(meta_base + n, cnt.at[x, z], cnt.at[x, z], dev_x[d])

    def meta2():
        for n, d in three:
            recv(meta_base + n, cnt.at[wrap(x - d), z], dev_x[d])
        for n, d in three:
            send(meta_base + 3 + n, cnt.at[:, z], cnt.at[:, z], dev_z[d])

    def meta():
        for n, d in three:
            recv(meta_base + 3 + n, cnt.at[:, wrap(z - d)], dev_z[d])

    tasks.update(meta1=meta1, meta2=meta2, meta=meta)

    def places(upto):
        total = jnp.zeros((8, 128), jnp.int32)
        found = []
        for b in range(upto):
            found.append([])
            for i in range(16):
                held = jnp.clip(cnt[i // 4, i % 4] - 16 * b, 0, 16)
                found[b].append((total, held))
                total = total + held
        return found

    def build_c(out, blocks, first_row):
        found = places(blocks[-1] + 1)
        lane = lax.broadcasted_iota(jnp.int32, (8, 128), 1)
        part_of, slot = lane // 16, lane % 16
        row = lax.broadcasted_iota(jnp.int32, (256, 128), 0) + first_row
        for b in blocks:
            for j in range(2):
                start, held = found[b][8 * j]
                for i in range(1, 8):
                    start = jnp.where(part_of == i, found[b][8 * j + i][0], start)
                    held = jnp.where(part_of == i, found[b][8 * j + i][1], held)
                place = jnp.where(slot < held, start + slot, -1)
                hit = jnp.broadcast_to(place[0:1], (256, 128)) == row
                at = 256 * (b - blocks[0]) + 128 * j
                out[:, at:at + 128] = jnp.where(hit, 1.0, 0.0).astype(BF)

    def buildc0():
        build_c(c_low, (0, 1), 0)

    def buildc1():
        build_c(c_high, (1, 2, 3), 256)

    def buildct():
        found = places(4)
        slot = lax.broadcasted_iota(jnp.int32, (16, 128), 0)
        lane = lax.broadcasted_iota(jnp.int32, (16, 128), 1)
        for i in range(16):
            for b in range(4):
                start = jnp.broadcast_to(found[b][i][0][0:1], (16, 128))
                held = jnp.broadcast_to(found[b][i][1][0:1], (16, 128))
                place = jnp.where(slot < held, start + slot, -1)
                for j in range(4):
                    hit = place == lane + 128 * j
                    ct[i // 4, i % 4, 16 * b:16 * b + 16, 128 * j:128 * j + 128] = jnp.where(
                        hit, 1.0, 0.0
                    ).astype(BF)

    tasks.update(buildc0=buildc0, buildc1=buildc1, buildct=buildct)

    def hidden_cols(core, yy, width=256):
        return pl.ds(pl.multiple_of(core * 1024 + yy * width, width), width)

    loaded = set()
    incoming = {}

    def add_chunk(t, k, r0, nr):
        mine = pl.ds(r0, nr)
        hr = nr // 2
        ic, io, inb = fresh(2), fresh(2), fresh(2)
        iy, iw, ih = fresh(2), fresh(2), fresh(4)
        far = lax.div(wrap(y + 2), 2)
        near = 1 - far

        def cmp():
            b0, b1 = (0 if r0 < 256 else 1), (r0 + nr) // 128
            width = 256 * (b1 - b0)
            at = r0 % 256
            picks = (c_low if r0 < 256 else c_high)[at:at + nr, :width]
            for h in range(2):
                got = dot(picks, ag[t, h, b0:b1].reshape(width, 512))
                rows[t, mine, 512 * h:512 * h + 512] = got.astype(BF)

        def pair(core, p):
            left = rows[t, mine, :]
            if t == 0:
                return dot(left, wi[:, hidden_cols(core, p, 512)])
            return dot(left, wo[hidden_cols(core, p, 512), :], NT)

        def for_other(p, n):
            got = pair(oc, p).astype(BF)
            xs[t, p, 0, mine] = got[:, :256]
            xs[t, p, 1, mine] = got[:, 256:]
            tiles = pl.ds(0, 2)
            send(ic + n, xs.at[t, p, tiles, mine], xr.at[t, p, tiles, mine], dev_c)

        def for_self(p, n):
            got = pair(c, p)
            recv(ic + n, xr.at[t, p, pl.ds(0, 2), mine], dev_c)
            acc[t, p, 0, mine] = got[:, :256] + xr[t, p, 0, mine].astype(F32)
            acc[t, p, 1, mine] = got[:, 256:] + xr[t, p, 1, mine].astype(F32)

        def tile(yy):
            return (t, lax.div(yy, 2), lax.rem(yy, 2), mine)

        def ma():
            if t not in loaded:
                loaded.add(t)
                load[t].wait()
            for_other(far, 0)

        def opp_landing(n):
            return (t, n, pl.ds(r0 // 2, hr))

        def mb():
            for_self(far, 0)
            ps[t, 0, mine] = acc[tile(wrap(y + 2))].astype(BF)
            for n, d in both:
                send(
                    io + n, ps.at[t, 0, pl.ds(r0 + hr * n, hr)], opp_rx.at[opp_landing(n)],
                    dev_y[d],
                )

        def mc():
            for_other(near, 1)

        def md():
            for_self(near, 1)

        def nb():
            for n, d in both:
                recv(io + n, opp_rx.at[opp_landing(n)], dev_y[d])
                got = acc[tile(wrap(y + d))]
                here = slice(hr * n, hr * n + hr)
                away = slice(hr - hr * n, nr - hr * n)
                added = got[here] + opp_rx[opp_landing(n)].astype(F32)
                ps[t, 1 + n, pl.ds(r0 + here.start, hr)] = added.astype(BF)
                ps[t, 1 + n, pl.ds(r0 + away.start, hr)] = got[away].astype(BF)
                send(inb + n, ps.at[t, 1 + n, mine], nbr_rx.at[t, n, mine], dev_y[d])

        def piece(core, yy):
            return hb.at[t, mine, hidden_cols(core, yy)]

        def half(yy, n):
            return hb.at[t, pl.ds(r0 + hr * n, hr), hidden_cols(c, yy)]

        def fin():
            for n, d in both:
                recv(inb + n, nbr_rx.at[t, n, mine], dev_y[d])
            total = acc[tile(y)] + nbr_rx[t, 0, mine].astype(F32) + nbr_rx[t, 1, mine].astype(F32)
            if t == 0:
                total, slopes = gelu_pair(total)
                slope[mine] = slopes
            else:
                total = total * slope[mine]
            hb[t, mine, hidden_cols(c, y)] = total.astype(BF)
            p = piece(c, y)
            send(iy, p, p, dev_y[1])
            send(iy + 1, p, p, dev_y[-1])
            send(ih, p, p, dev_c)

        def fwd():
            for n, d in both:
                p, q = piece(c, wrap(y - d)), half(wrap(y - d), n)
                recv(iy + n, p, dev_y[d])
                send(iw + n, q, q, dev_y[d])
                send(ih + 1 + n, p, p, dev_c)

        def opp():
            for n, d in both:
                recv(iw + n, half(wrap(y + 2), n), dev_y[d])
            p = piece(c, wrap(y + 2))
            send(ih + 3, p, p, dev_c)

        def near_in():
            for n, yy in enumerate((y, wrap(y - 1), wrap(y + 1))):
                recv(ih + n, piece(oc, yy), dev_c)

        def far_in():
            recv(ih + 3, piece(oc, wrap(y + 2)), dev_c)

        incoming.setdefault((t, r0 // 256), []).append((near_in, far_in))
        for f in (cmp, ma, mb, mc, md, nb, fin, fwd, opp):
            tasks[f"{f.__name__}_{t}{k}"] = f

    def add_contract(t, half):
        mine = pl.ds(256 * half, 256)
        arrivals = incoming[t, half]

        def whole():
            for near_in, far_in in arrivals:
                near_in()
                far_in()

            def step(n, carry):
                cols = pl.ds(pl.multiple_of(n * 512, 512), 512)
                left = hb[t, mine, :]
                got = dot(left, wo[:, cols]) if t == 0 else dot(left, wi[cols, :], NT)
                part[t, mine, cols] = got.astype(BF)
                return carry

            lax.fori_loop(0, 2, step, 0)

        def product(core, yy):
            units = hidden_cols(core, yy)
            left = hb[t, mine, units]
            return dot(left, wo[units, :]) if t == 0 else dot(left, wi[:, units], NT)

        def ct1():
            for near_in, far_in in arrivals[:-1]:
                near_in()
                far_in()
            arrivals[-1][0]()
            sub[...] = product(c, y)

            def step(n, carry):
                core = lax.rem(c + lax.div(n + 2, 4), 2)
                away = lax.div(n + 2, 4) * (n + 1) + (1 - lax.div(n + 2, 4)) * (2 * n + 3)
                sub[...] += product(core, wrap(y + away))
                return carry

            lax.fori_loop(0, 5, step, 0)

        def ct2():
            sub[...] += product(c, wrap(y + 2))
            arrivals[-1][1]()
            part[t, mine, :] = (sub[...] + product(oc, wrap(y + 2))).astype(BF)

        if (t, half) == (1, 1):
            tasks["ct1_11"], tasks["ct2_11"] = ct1, ct2
        else:
            tasks[f"ct_{t}{half}"] = whole

    def add_home(t):
        tag = ("m", "d1")[t]
        base = [fresh(19), fresh(19)]

        def group(h, fi):
            picks = ct[fi] if h == 0 else ct[:, fi]
            got = dot(picks.reshape(256, 512), part[t, :, 512 * h:512 * h + 512])
            return got.reshape(4, 64, 512)

        def e0():
            for h in range(2):
                f, s, fd, sd = axes(h)
                spread[t, h, 0] = group(h, wrap(f + 2)).astype(BF)
                for q, far in enumerate((2, 1, -1, 0)):
                    to = wrap(s + far)
                    for n, d in both:
                        send(
                            base[h] + 2 * q + n, spread.at[t, h, 0, to, pl.ds(32 * n, 32)],
                            f_opp.at[t, h, q, n], fd[d],
                        )

        def e1():
            for h in range(2):
                f, s, fd, sd = axes(h)
                for n, d in both:
                    spread[t, h, 1 + n] = group(h, wrap(f + d)).astype(BF)

        def e2():
            for h in range(2):
                home[t, h] = group(h, axes(h)[0])

        def fn(q, far):
            def run():
                for h in range(2):
                    f, s, fd, sd = axes(h)
                    to = wrap(s + far)
                    for n, d in both:
                        recv(base[h] + 2 * q + n, f_opp.at[t, h, q, n], fd[d])
                        here = slice(32 * n, 32 * n + 32)
                        spread[t, h, 1 + n, to, here] = (
                            spread[t, h, 1 + n, to, here].astype(F32)
                            + f_opp[t, h, q, n].astype(F32)
                        ).astype(BF)
                        send(
                            base[h] + 8 + 2 * q + n, spread.at[t, h, 1 + n, to],
                            f_nbr.at[t, h, q, n], fd[d],
                        )
            return run

        def fs(q, far):
            def run():
                for h in range(2):
                    f, s, fd, sd = axes(h)
                    to = wrap(s + far)
                    for n, d in both:
                        recv(base[h] + 8 + 2 * q + n, f_nbr.at[t, h, q, n], fd[d])
                    got = (
                        home[t, h, to]
                        + f_nbr[t, h, q, 0].astype(F32)
                        + f_nbr[t, h, q, 1].astype(F32)
                    )
                    if q == 3:
                        home[t, h, to] = got
                    else:
                        grouped[t, h, q] = got.astype(BF)
                        send(
                            base[h] + 16 + q, grouped.at[t, h, q], s_rx.at[t, h, q], sd[far]
                        )
            return run

        def g3():
            for h in range(2):
                f, s, fd, sd = axes(h)
                got = home[t, h, s]
                for q, far in enumerate((2, 1, -1)):
                    recv(base[h] + 16 + q, s_rx.at[t, h, q], sd[far])
                    got = got + s_rx[t, h, q].astype(F32)
                if t == 0:
                    got = gate[:, 0:1] * got
                slots_out[t, :, 512 * h:512 * h + 512] = got.astype(BF)

        for f in (e0, e1, e2, g3):
            tasks[f"{f.__name__}_{tag}"] = f
        for q, far in enumerate((2, 1, -1, 0)):
            tasks[f"fn{q}_{tag}"] = fn(q, far)
            tasks[f"fs{q}_{tag}"] = fs(q, far)

    moved = {}

    def dwo_tile(j):
        def run():
            here = pl.ds(256 * j, 256)
            got = dot(hb[0, :, here], rows[1], TN).astype(BF)
            if j >= 2:
                moved["o", j - 2].wait()
            dwo[j % 2] = got
            moved["o", j] = local_copy(dwo.at[j % 2], dwo_out.at[here])
        return run

    def dwi_tile(j):
        def run():
            here = pl.ds(256 * j, 256)
            got = dot(rows[0, :, here], hb[1], TN).astype(BF)
            if j >= 2:
                moved["i", j - 2].wait()
            dwi[j % 2] = got
            moved["i", j] = local_copy(dwi.at[j % 2], dwi_out.at[here])
        return run

    for j in range(8):
        tasks[f"dwo{j}"] = dwo_tile(j)
    for j in range(4):
        tasks[f"dwi{j}"] = dwi_tile(j)
    for t in range(2):
        for ph, (b0, nb) in enumerate(PHASES[t]):
            add_gather(t, ph, b0, nb)
        for k, (r0, nr) in enumerate(CHUNKS[t]):
            add_chunk(t, k, r0, nr)
        for half in range(2):
            add_contract(t, half)
        add_home(t)

    entered = False
    for name in ORDER:
        if name == "ag1_00":
            pl.semaphore_wait(barrier, len(partners))
            entered = True
        assert entered or name.startswith("pick")
        tasks.pop(name)()
    assert not tasks

    for d in sent:
        d.wait_send()
    for j in (6, 7):
        moved["o", j].wait()
    for j in (2, 3):
        moved["i", j].wait()


def exchange(chosen, gates, counts, tokens, cotangent, w_in, w_out):
    vmem = pl.BlockSpec(memory_space=pltpu.VMEM)
    anywhere = pl.BlockSpec(memory_space=pl.ANY)
    hbm = pl.BlockSpec(memory_space=pltpu.HBM)

    def v(*shape, dtype=BF):
        return pltpu.VMEM(shape, dtype)

    return pl.pallas_call(
        kernel,
        out_shape=(
            pltpu.VMEM((64, 256), BF),
            pltpu.VMEM((2, 64, 1024), BF),
            pltpu.VMEM((1024, 2048), BF),
            pltpu.VMEM((2048, 1024), BF),
        ),
        in_specs=[vmem] * 3 + [hbm] * 4,
        out_specs=(vmem, vmem, anywhere, anywhere),
        scratch_shapes=[
            v(256, 1024), v(256, 1024), v(1024, 2048), v(2048, 1024),
            v(64, 128, dtype=F32),
            v(2, 2, 4, 4, 4, 16, 512),
            v(4, 4, 8, 128, dtype=jnp.int32),
            v(256, 512), v(256, 768),
            v(4, 4, 64, 512),
            v(2, 512, 1024),
            v(2, 2, 2, 512, 256), v(2, 2, 2, 512, 256),
            v(2, 3, 512, 256),
            v(2, 2, 256, 256),
            v(2, 2, 512, 256),
            v(2, 2, 2, 512, 256, dtype=F32),
            v(512, 256, dtype=F32),
            v(2, 512, 2048),
            v(256, 1024, dtype=F32),
            v(2, 512, 1024),
            v(2, 2, 3, 4, 64, 512),
            v(2, 2, 4, 64, 512, dtype=F32),
            v(2, 2, 4, 2, 32, 512),
            v(2, 2, 4, 2, 64, 512),
            v(2, 2, 3, 64, 512),
            v(2, 2, 3, 64, 512),
            v(2, 256, 2048), v(2, 256, 1024),
            pltpu.SemaphoreType.DMA((N_COPIES,)),
            pltpu.SemaphoreType.DMA((N_COPIES,)),
            pltpu.SemaphoreType.DMA((N_LOCAL,)),
        ],
        compiler_params=pltpu.CompilerParams(
            collective_id=0, has_side_effects=True, vmem_limit_bytes=54 * 2**20
        ),
        cost_estimate=pl.CostEstimate(
            flops=14 * 10**9, bytes_accessed=20 * 2**20, transcendentals=2**19
        ),
    )(chosen, gates, counts, tokens, cotangent, w_in, w_out)


def finish_kernel(
    pick_ref, slots_ref, dwi_in, dwo_in, mixed_out, d_tok_out, dwi_out, dwo_out, spot, sem
):
    moves = []
    for src, dst, n in ((dwi_in, dwi_out, 256), (dwo_in, dwo_out, 512)):
        for j in range(4):
            here = pl.ds(n * j, n)
            d = pltpu.make_async_copy(src.at[here], dst.at[here], sem.at[len(moves)])
            d.start()
            moves.append(d)
    for t, out in enumerate((mixed_out, d_tok_out)):
        spot[t] = dot(pick_ref[...], slots_ref[t], TN).astype(BF)
        d = pltpu.make_async_copy(spot.at[t], out, sem.at[len(moves)])
        d.start()
        moves.append(d)
    for d in moves:
        d.wait()


def finish(pick, slots, d_w_in, d_w_out):
    vmem = pl.BlockSpec(memory_space=pltpu.VMEM)
    anywhere = pl.BlockSpec(memory_space=pl.ANY)
    hbm = pl.BlockSpec(memory_space=pltpu.HBM)
    return pl.pallas_call(
        finish_kernel,
        out_shape=(
            jax.ShapeDtypeStruct((256, 1024), BF),
            jax.ShapeDtypeStruct((256, 1024), BF),
            jax.ShapeDtypeStruct((1024, 2048), BF),
            jax.ShapeDtypeStruct((2048, 1024), BF),
        ),
        in_specs=[vmem, vmem, anywhere, anywhere],
        out_specs=(hbm, hbm, hbm, hbm),
        scratch_shapes=[pltpu.VMEM((2, 256, 1024), BF), pltpu.SemaphoreType.DMA((10,))],
        compiler_params=pltpu.CompilerParams(vmem_limit_bytes=8 * 2**20),
        cost_estimate=pl.CostEstimate(
            flops=6 * 10**7, bytes_accessed=18 * 2**20, transcendentals=0
        ),
    )(pick, slots, d_w_in, d_w_out)


def local(tokens, w_in, w_out, chosen, counts, gates, cotangent):
    return finish(*exchange(chosen, gates, counts.reshape(1, 1), tokens, cotangent, w_in, w_out))


def solution(mesh):
    in_specs = (
        P("dp", "expert"),
        P("expert", "dp"),
        P("dp", "expert"),
        P("dp", None),
        P("dp"),
        P("dp", None),
        P("dp", "expert"),
    )
    out_specs = (P("dp", "expert"), P("dp", "expert"), P("expert", "dp"), P("dp", "expert"))
    return jax.shard_map(local, mesh=mesh, in_specs=in_specs, out_specs=out_specs, check_vma=False)
```

```python
import jax
import jax.numpy as jnp
from jax import lax
from jax.experimental import pallas as pl
from jax.experimental.pallas import tpu as pltpu
from jax.sharding import PartitionSpec as P

half_root = 0.7071067811865476
inv_root_tau = 0.3989422804014327

MESH = pl.DeviceIdType.MESH
BF = jnp.bfloat16
F32 = jnp.float32

N_COPIES = 300
N_LOCAL = 24

CHUNKS = ([(0, 128), (128, 128), (256, 128), (384, 128)], [(0, 256), (256, 256)])
PHASES = ([(0, 1), (1, 1), (2, 1), (3, 1)], [(0, 2), (2, 2)])

ORDER = (
    "pick0", "ag1_00", "meta1", "pick1", "ag1_02", "ag1_03", "ag1_01", "meta2", "ag2_00",
    "ag2_01", "ag2_02", "ag2_03", "meta", "buildc1", "buildc0", "ag3_00", "ag4_00", "cmp_00",
    "ma_00", "ag3_01", "ag1_10", "mb_00", "mc_00", "ag3_02", "ag1_11", "md_00", "ag4_01",
    "cmp_01", "ma_01", "ag3_03", "nb_00", "mb_01", "ag4_02", "cmp_02", "ma_02", "ag2_10", "mc_01",
    "mb_02", "ag2_11", "ag4_03", "cmp_03", "md_01", "nb_01", "fin_00", "ma_03", "mc_02", "mb_03",
    "ag3_10", "md_02", "nb_02", "mc_03", "fin_01", "ag3_11", "md_03", "nb_03", "fwd_00", "ag4_10",
    "cmp_10", "ma_10", "fin_02", "mb_10", "ag4_11", "cmp_11", "fin_03", "ma_11", "mc_10",
    "opp_00", "fwd_02", "fwd_01", "mb_11", "mc_11", "md_10", "fwd_03", "nb_10", "opp_02", "md_11",
    "opp_01", "buildct", "nb_11", "opp_03", "ct_00", "fin_10", "ct_01", "fin_11", "e0_m", "e1_m",
    "fwd_10", "dwo0", "dwo1", "e2_m", "fn0_m", "fn1_m", "fwd_11", "dwo2", "fn2_m", "fn3_m",
    "opp_10", "ct1_11", "fs0_m", "opp_11", "ct_10", "fs1_m", "fs2_m", "ct2_11", "e0_d1", "dwi0",
    "fs3_m", "e1_d1", "fn0_d1", "fn1_d1", "e2_d1", "fn2_d1", "fn3_d1", "dwo3", "dwi1", "dwo4",
    "dwo5", "fs0_d1", "fs1_d1", "dwo6", "g3_m", "fs2_d1", "dwo7", "dwi2", "dwi3", "fs3_d1",
    "g3_d1",
)

NN = (((1,), (0,)), ((), ()))
NT = (((1,), (1,)), ((), ()))
TN = (((0,), (0,)), ((), ()))


def dot(a, b, dims=NN):
    return lax.dot_general(a, b, dims, preferred_element_type=F32)


def gelu_pair(pre_act):
    cdf_part = 0.5 * (1.0 + lax.erf(pre_act * half_root))
    slopes = cdf_part + pre_act * jnp.exp(-0.5 * pre_act * pre_act) * inv_root_tau
    return (pre_act * cdf_part, slopes)


def wrap(v):
    return lax.rem(v + 8, 4)


def kernel(
    chosen_ref, gates_ref, count_ref, tok_hbm, cot_hbm, wi_hbm, wo_hbm,
    pick_out, slots_out, dwi_out, dwo_out,
    tok, cot, wi, wo, gate, ag, cnt, c_low, c_high, ct, rows, xs, xr, ps, opp_rx, nbr_rx, acc, slope, hb,
    sub, part, spread, home, f_opp, f_nbr, grouped, s_rx, dwi, dwo,
    send_sem, recv_sem, local_sem,
):
    dp, ex = lax.axis_index("dp"), lax.axis_index("expert")
    x, z = lax.div(dp, 4), lax.rem(dp, 4)
    y, c = lax.div(ex, 2), lax.rem(ex, 2)
    oc = 1 - c
    dev_x = {d: (wrap(x + d) * 4 + z, ex) for d in (1, -1, 2)}
    dev_z = {d: (x * 4 + wrap(z + d), ex) for d in (1, -1, 2)}
    dev_y = {d: (dp, wrap(y + d) * 2 + c) for d in (1, -1)}
    dev_c = (dp, y * 2 + oc)
    both = ((0, 1), (1, -1))
    three = ((0, 1), (1, -1), (2, 2))

    counter = [0]
    sent = []

    def fresh(n):
        first = counter[0]
        counter[0] += n
        assert counter[0] <= N_COPIES
        return first

    def copy(i, src, dst, dev):
        return pltpu.make_async_remote_copy(
            src_ref=src, dst_ref=dst, send_sem=send_sem.at[i], recv_sem=recv_sem.at[i],
            device_id=dev, device_id_type=MESH,
        )

    def send(i, src, dst, dev):
        d = copy(i, src, dst, dev)
        d.start()
        sent.append(d)

    def recv(i, landing, dev):
        copy(i, landing, landing, dev).wait_recv()

    opened = []

    def local_copy(src, dst):
        d = pltpu.make_async_copy(src, dst, local_sem.at[len(opened)])
        d.start()
        opened.append(d)
        return d

    load = {
        "tok": local_copy(tok_hbm, tok),
        "cot": local_copy(cot_hbm, cot),
        0: local_copy(wi_hbm, wi),
        1: local_copy(wo_hbm, wo),
    }

    barrier = pltpu.get_barrier_semaphore()
    partners = [dev_x[d] for d in dev_x] + [dev_z[d] for d in dev_z] + [dev_y[1], dev_y[-1], dev_c]
    for dev in partners:
        pl.semaphore_signal(barrier, inc=1, device_id=dev, device_id_type=MESH)

    tasks = {}

    def column(row):
        here = lax.broadcasted_iota(jnp.int32, (64, 64), 0)
        there = lax.broadcasted_iota(jnp.int32, (64, 64), 1)
        wide = jnp.broadcast_to(row.astype(F32), (64, 64))
        return jnp.sum(jnp.where(here == there, wide, 0.0), axis=1, keepdims=True)

    def pick0():
        place = jnp.broadcast_to(column(chosen_ref[...]), (64, 256)).astype(jnp.int32)
        spot = lax.broadcasted_iota(jnp.int32, (64, 256), 1)
        slot = lax.broadcasted_iota(jnp.int32, (64, 256), 0)
        held = jnp.broadcast_to(count_ref[...], (64, 256))
        hit = jnp.where(place == spot, 1.0, 0.0) * jnp.where(slot < held, 1.0, 0.0)
        pick_out[...] = hit.astype(BF)
        gate[...] = jnp.broadcast_to(column(gates_ref[...]), (64, 128))
        cnt[x, z] = jnp.broadcast_to(count_ref[...], (8, 128))
        load["tok"].wait()
        keep(0, dot(pick_out[...], tok[...]).astype(BF))

    def pick1():
        load["cot"].wait()
        keep(1, (gate[:, 0:1] * dot(pick_out[...], cot[...])).astype(BF))

    def keep(t, got):
        for b in range(4):
            for h in range(2):
                ag[t, h, b, x, z] = got[16 * b:16 * b + 16, 512 * h:512 * h + 512]

    tasks["pick0"], tasks["pick1"] = pick0, pick1

    def axes(h):
        return (x, z, dev_x, dev_z) if h == 0 else (z, x, dev_z, dev_x)

    def add_gather(t, ph, b0, nb):
        base = [fresh(8), fresh(8)]
        blocks = pl.ds(b0, nb)
        direct = (t, ph) == (0, 0)

        def blk(h, fi, si):
            return ag.at[(t, h, blocks) + ((fi, si) if h == 0 else (si, fi))]

        def grp(h, si, first, n):
            many = pl.ds(first, n)
            return ag.at[(t, h, blocks) + ((many, si) if h == 0 else (si, many))]

        def ag1():
            for h in range(2):
                f, s, fd, sd = axes(h)
                for n, d in three:
                    send(base[h] + n, blk(h, f, s), blk(h, f, s), fd[d])

        def ag2():
            for h in range(2):
                f, s, fd, sd = axes(h)
                for n, d in three:
                    recv(base[h] + n, blk(h, wrap(f - d), s), fd[d])
                for n, d in three if direct else both:
                    send(base[h] + 3 + n, grp(h, s, 0, 4), grp(h, s, 0, 4), sd[d])

        def ag3():
            for h in range(2):
                f, s, fd, sd = axes(h)
                for n, d in three if direct else both:
                    recv(base[h] + 3 + n, grp(h, wrap(s - d), 0, 4), sd[d])
                    if not direct:
                        g = grp(h, wrap(s - d), 2 * n, 2)
                        send(base[h] + 6 + n, g, g, sd[d])

        def ag4():
            for h in range(2):
                f, s, fd, sd = axes(h)
                for n, d in both:
                    if not direct:
                        recv(base[h] + 6 + n, grp(h, wrap(s + 2), 2 * n, 2), sd[d])

        for name, f in (("ag1", ag1), ("ag2", ag2), ("ag3", ag3), ("ag4", ag4)):
            tasks[f"{name}_{t}{ph}"] = f

    meta_base = fresh(6)

    def meta1():
        for n, d in three:
            send(meta_base + n, cnt.at[x, z], cnt.at[x, z], dev_x[d])

    def meta2():
        for n, d in three:
            recv(meta_base + n, cnt.at[wrap(x - d), z], dev_x[d])
        for n, d in three:
            send(meta_base + 3 + n, cnt.at[:, z], cnt.at[:, z], dev_z[d])

    def meta():
        for n, d in three:
            recv(meta_base + 3 + n, cnt.at[:, wrap(z - d)], dev_z[d])

    tasks.update(meta1=meta1, meta2=meta2, meta=meta)

    def places(upto):
        total = jnp.zeros((8, 128), jnp.int32)
        found = []
        for b in range(upto):
            found.append([])
            for i in range(16):
                held = jnp.clip(cnt[i // 4, i % 4] - 16 * b, 0, 16)
                found[b].append((total, held))
                total = total + held
        return found

    def build_c(out, blocks, first_row):
        found = places(blocks[-1] + 1)
        lane = lax.broadcasted_iota(jnp.int32, (8, 128), 1)
        part_of, slot = lane // 16, lane % 16
        row = lax.broadcasted_iota(jnp.int32, (256, 128), 0) + first_row
        for b in blocks:
            for j in range(2):
                start, held = found[b][8 * j]
                for i in range(1, 8):
                    start = jnp.where(part_of == i, found[b][8 * j + i][0], start)
                    held = jnp.where(part_of == i, found[b][8 * j + i][1], held)
                place = jnp.where(slot < held, start + slot, -1)
                hit = jnp.broadcast_to(place[0:1], (256, 128)) == row
                at = 256 * (b - blocks[0]) + 128 * j
                out[:, at:at + 128] = jnp.where(hit, 1.0, 0.0).astype(BF)

    def buildc0():
        build_c(c_low, (0, 1), 0)

    def buildc1():
        build_c(c_high, (1, 2, 3), 256)

    def buildct():
        found = places(4)
        slot = lax.broadcasted_iota(jnp.int32, (16, 128), 0)
        lane = lax.broadcasted_iota(jnp.int32, (16, 128), 1)
        for i in range(16):
            for b in range(4):
                start = jnp.broadcast_to(found[b][i][0][0:1], (16, 128))
                held = jnp.broadcast_to(found[b][i][1][0:1], (16, 128))
                place = jnp.where(slot < held, start + slot, -1)
                for j in range(4):
                    hit = place == lane + 128 * j
                    ct[i // 4, i % 4, 16 * b:16 * b + 16, 128 * j:128 * j + 128] = jnp.where(
                        hit, 1.0, 0.0
                    ).astype(BF)

    tasks.update(buildc0=buildc0, buildc1=buildc1, buildct=buildct)

    def hidden_cols(core, yy, width=256):
        return pl.ds(pl.multiple_of(core * 1024 + yy * width, width), width)

    loaded = set()
    incoming = {}

    def add_chunk(t, k, r0, nr):
        mine = pl.ds(r0, nr)
        hr = nr // 2
        ic, io, inb = fresh(2), fresh(2), fresh(2)
        iy, iw, ih = fresh(2), fresh(2), fresh(4)
        far = lax.div(wrap(y + 2), 2)
        near = 1 - far

        def cmp():
            b0, b1 = (0 if r0 < 256 else 1), (r0 + nr) // 128
            width = 256 * (b1 - b0)
            at = r0 % 256
            picks = (c_low if r0 < 256 else c_high)[at:at + nr, :width]
            for h in range(2):
                got = dot(picks, ag[t, h, b0:b1].reshape(width, 512))
                rows[t, mine, 512 * h:512 * h + 512] = got.astype(BF)

        def pair(core, p):
            left = rows[t, mine, :]
            if t == 0:
                return dot(left, wi[:, hidden_cols(core, p, 512)])
            return dot(left, wo[hidden_cols(core, p, 512), :], NT)

        def for_other(p, n):
            got = pair(oc, p).astype(BF)
            xs[t, p, 0, mine] = got[:, :256]
            xs[t, p, 1, mine] = got[:, 256:]
            tiles = pl.ds(0, 2)
            send(ic + n, xs.at[t, p, tiles, mine], xr.at[t, p, tiles, mine], dev_c)

        def for_self(p, n):
            got = pair(c, p)
            recv(ic + n, xr.at[t, p, pl.ds(0, 2), mine], dev_c)
            acc[t, p, 0, mine] = got[:, :256] + xr[t, p, 0, mine].astype(F32)
            acc[t, p, 1, mine] = got[:, 256:] + xr[t, p, 1, mine].astype(F32)

        def tile(yy):
            return (t, lax.div(yy, 2), lax.rem(yy, 2), mine)

        def ma():
            if t not in loaded:
                loaded.add(t)
                load[t].wait()
            for_other(far, 0)

        def opp_landing(n):
            return (t, n, pl.ds(r0 // 2, hr))

        def mb():
            for_self(far, 0)
            ps[t, 0, mine] = acc[tile(wrap(y + 2))].astype(BF)
            for n, d in both:
                send(
                    io + n, ps.at[t, 0, pl.ds(r0 + hr * n, hr)], opp_rx.at[opp_landing(n)],
                    dev_y[d],
                )

        def mc():
            for_other(near, 1)

        def md():
            for_self(near, 1)

        def nb():
            for n, d in both:
                recv(io + n, opp_rx.at[opp_landing(n)], dev_y[d])
                got = acc[tile(wrap(y + d))]
                here = slice(hr * n, hr * n + hr)
                away = slice(hr - hr * n, nr - hr * n)
                added = got[here] + opp_rx[opp_landing(n)].astype(F32)
                ps[t, 1 + n, pl.ds(r0 + here.start, hr)] = added.astype(BF)
                ps[t, 1 + n, pl.ds(r0 + away.start, hr)] = got[away].astype(BF)
                send(inb + n, ps.at[t, 1 + n, mine], nbr_rx.at[t, n, mine], dev_y[d])

        def piece(core, yy):
            return hb.at[t, mine, hidden_cols(core, yy)]

        def half(yy, n):
            return hb.at[t, pl.ds(r0 + hr * n, hr), hidden_cols(c, yy)]

        def fin():
            for n, d in both:
                recv(inb + n, nbr_rx.at[t, n, mine], dev_y[d])
            total = acc[tile(y)] + nbr_rx[t, 0, mine].astype(F32) + nbr_rx[t, 1, mine].astype(F32)
            if t == 0:
                total, slopes = gelu_pair(total)
                slope[mine] = slopes
            else:
                total = total * slope[mine]
            hb[t, mine, hidden_cols(c, y)] = total.astype(BF)
            p = piece(c, y)
            send(iy, p, p, dev_y[1])
            send(iy + 1, p, p, dev_y[-1])
            send(ih, p, p, dev_c)

        def fwd():
            for n, d in both:
                p, q = piece(c, wrap(y - d)), half(wrap(y - d), n)
                recv(iy + n, p, dev_y[d])
                send(iw + n, q, q, dev_y[d])
                send(ih + 1 + n, p, p, dev_c)

        def opp():
            for n, d in both:
                recv(iw + n, half(wrap(y + 2), n), dev_y[d])
            p = piece(c, wrap(y + 2))
            send(ih + 3, p, p, dev_c)

        def near_in():
            for n, yy in enumerate((y, wrap(y - 1), wrap(y + 1))):
                recv(ih + n, piece(oc, yy), dev_c)

        def far_in():
            recv(ih + 3, piece(oc, wrap(y + 2)), dev_c)

        incoming.setdefault((t, r0 // 256), []).append((near_in, far_in))
        for f in (cmp, ma, mb, mc, md, nb, fin, fwd, opp):
            tasks[f"{f.__name__}_{t}{k}"] = f

    def add_contract(t, half):
        mine = pl.ds(256 * half, 256)
        arrivals = incoming[t, half]

        def whole():
            for near_in, far_in in arrivals:
                near_in()
                far_in()

            def step(n, carry):
                cols = pl.ds(pl.multiple_of(n * 512, 512), 512)
                left = hb[t, mine, :]
                got = dot(left, wo[:, cols]) if t == 0 else dot(left, wi[cols, :], NT)
                part[t, mine, cols] = got.astype(BF)
                return carry

            lax.fori_loop(0, 2, step, 0)

        def product(core, yy):
            units = hidden_cols(core, yy)
            left = hb[t, mine, units]
            return dot(left, wo[units, :]) if t == 0 else dot(left, wi[:, units], NT)

        def ct1():
            for near_in, far_in in arrivals[:-1]:
                near_in()
                far_in()
            arrivals[-1][0]()
            sub[...] = product(c, y)

            def step(n, carry):
                core = lax.rem(c + lax.div(n + 2, 4), 2)
                away = lax.div(n + 2, 4) * (n + 1) + (1 - lax.div(n + 2, 4)) * (2 * n + 3)
                sub[...] += product(core, wrap(y + away))
                return carry

            lax.fori_loop(0, 5, step, 0)

        def ct2():
            sub[...] += product(c, wrap(y + 2))
            arrivals[-1][1]()
            part[t, mine, :] = (sub[...] + product(oc, wrap(y + 2))).astype(BF)

        if (t, half) == (1, 1):
            tasks["ct1_11"], tasks["ct2_11"] = ct1, ct2
        else:
            tasks[f"ct_{t}{half}"] = whole

    def add_home(t):
        tag = ("m", "d1")[t]
        base = [fresh(19), fresh(19)]

        def group(h, fi):
            picks = ct[fi] if h == 0 else ct[:, fi]
            got = dot(picks.reshape(256, 512), part[t, :, 512 * h:512 * h + 512])
            return got.reshape(4, 64, 512)

        def e0():
            for h in range(2):
                f, s, fd, sd = axes(h)
                spread[t, h, 0] = group(h, wrap(f + 2)).astype(BF)
                for q, far in enumerate((2, 1, -1, 0)):
                    to = wrap(s + far)
                    for n, d in both:
                        send(
                            base[h] + 2 * q + n, spread.at[t, h, 0, to, pl.ds(32 * n, 32)],
                            f_opp.at[t, h, q, n], fd[d],
                        )

        def e1():
            for h in range(2):
                f, s, fd, sd = axes(h)
                for n, d in both:
                    spread[t, h, 1 + n] = group(h, wrap(f + d)).astype(BF)

        def e2():
            for h in range(2):
                home[t, h] = group(h, axes(h)[0])

        def fn(q, far):
            def run():
                for h in range(2):
                    f, s, fd, sd = axes(h)
                    to = wrap(s + far)
                    for n, d in both:
                        recv(base[h] + 2 * q + n, f_opp.at[t, h, q, n], fd[d])
                        here = slice(32 * n, 32 * n + 32)
                        spread[t, h, 1 + n, to, here] = (
                            spread[t, h, 1 + n, to, here].astype(F32)
                            + f_opp[t, h, q, n].astype(F32)
                        ).astype(BF)
                        send(
                            base[h] + 8 + 2 * q + n, spread.at[t, h, 1 + n, to],
                            f_nbr.at[t, h, q, n], fd[d],
                        )
            return run

        def fs(q, far):
            def run():
                for h in range(2):
                    f, s, fd, sd = axes(h)
                    to = wrap(s + far)
                    for n, d in both:
                        recv(base[h] + 8 + 2 * q + n, f_nbr.at[t, h, q, n], fd[d])
                    got = (
                        home[t, h, to]
                        + f_nbr[t, h, q, 0].astype(F32)
                        + f_nbr[t, h, q, 1].astype(F32)
                    )
                    if q == 3:
                        home[t, h, to] = got
                    else:
                        grouped[t, h, q] = got.astype(BF)
                        send(
                            base[h] + 16 + q, grouped.at[t, h, q], s_rx.at[t, h, q], sd[far]
                        )
            return run

        def g3():
            for h in range(2):
                f, s, fd, sd = axes(h)
                got = home[t, h, s]
                for q, far in enumerate((2, 1, -1)):
                    recv(base[h] + 16 + q, s_rx.at[t, h, q], sd[far])
                    got = got + s_rx[t, h, q].astype(F32)
                if t == 0:
                    got = gate[:, 0:1] * got
                slots_out[t, :, 512 * h:512 * h + 512] = got.astype(BF)

        for f in (e0, e1, e2, g3):
            tasks[f"{f.__name__}_{tag}"] = f
        for q, far in enumerate((2, 1, -1, 0)):
            tasks[f"fn{q}_{tag}"] = fn(q, far)
            tasks[f"fs{q}_{tag}"] = fs(q, far)

    moved = {}

    def dwo_tile(j):
        def run():
            here = pl.ds(256 * j, 256)
            got = dot(hb[0, :, here], rows[1], TN).astype(BF)
            if j >= 2:
                moved["o", j - 2].wait()
            dwo[j % 2] = got
            moved["o", j] = local_copy(dwo.at[j % 2], dwo_out.at[here])
        return run

    def dwi_tile(j):
        def run():
            here = pl.ds(256 * j, 256)
            got = dot(rows[0, :, here], hb[1], TN).astype(BF)
            if j >= 2:
                moved["i", j - 2].wait()
            dwi[j % 2] = got
            moved["i", j] = local_copy(dwi.at[j % 2], dwi_out.at[here])
        return run

    for j in range(8):
        tasks[f"dwo{j}"] = dwo_tile(j)
    for j in range(4):
        tasks[f"dwi{j}"] = dwi_tile(j)
    for t in range(2):
        for ph, (b0, nb) in enumerate(PHASES[t]):
            add_gather(t, ph, b0, nb)
        for k, (r0, nr) in enumerate(CHUNKS[t]):
            add_chunk(t, k, r0, nr)
        for half in range(2):
            add_contract(t, half)
        add_home(t)

    entered = False
    for name in ORDER:
        if name == "ag1_00":
            pl.semaphore_wait(barrier, len(partners))
            entered = True
        assert entered or name.startswith("pick")
        tasks.pop(name)()
    assert not tasks

    for d in sent:
        d.wait_send()
    for j in (6, 7):
        moved["o", j].wait()
    for j in (2, 3):
        moved["i", j].wait()


def exchange(chosen, gates, counts, tokens, cotangent, w_in, w_out):
    vmem = pl.BlockSpec(memory_space=pltpu.VMEM)
    anywhere = pl.BlockSpec(memory_space=pl.ANY)
    hbm = pl.BlockSpec(memory_space=pltpu.HBM)

    def v(*shape, dtype=BF):
        return pltpu.VMEM(shape, dtype)

    return pl.pallas_call(
        kernel,
        out_shape=(
            pltpu.VMEM((64, 256), BF),
            pltpu.VMEM((2, 64, 1024), BF),
            pltpu.VMEM((1024, 2048), BF),
            pltpu.VMEM((2048, 1024), BF),
        ),
        in_specs=[vmem] * 3 + [hbm] * 4,
        out_specs=(vmem, vmem, anywhere, anywhere),
        scratch_shapes=[
            v(256, 1024), v(256, 1024), v(1024, 2048), v(2048, 1024),
            v(64, 128, dtype=F32),
            v(2, 2, 4, 4, 4, 16, 512),
            v(4, 4, 8, 128, dtype=jnp.int32),
            v(256, 512), v(256, 768),
            v(4, 4, 64, 512),
            v(2, 512, 1024),
            v(2, 2, 2, 512, 256), v(2, 2, 2, 512, 256),
            v(2, 3, 512, 256),
            v(2, 2, 256, 256),
            v(2, 2, 512, 256),
            v(2, 2, 2, 512, 256, dtype=F32),
            v(512, 256, dtype=F32),
            v(2, 512, 2048),
            v(256, 1024, dtype=F32),
            v(2, 512, 1024),
            v(2, 2, 3, 4, 64, 512),
            v(2, 2, 4, 64, 512, dtype=F32),
            v(2, 2, 4, 2, 32, 512),
            v(2, 2, 4, 2, 64, 512),
            v(2, 2, 3, 64, 512),
            v(2, 2, 3, 64, 512),
            v(2, 256, 2048), v(2, 256, 1024),
            pltpu.SemaphoreType.DMA((N_COPIES,)),
            pltpu.SemaphoreType.DMA((N_COPIES,)),
            pltpu.SemaphoreType.DMA((N_LOCAL,)),
        ],
        compiler_params=pltpu.CompilerParams(
            collective_id=0, has_side_effects=True, vmem_limit_bytes=54 * 2**20
        ),
        cost_estimate=pl.CostEstimate(
            flops=14 * 10**9, bytes_accessed=20 * 2**20, transcendentals=2**19
        ),
    )(chosen, gates, counts, tokens, cotangent, w_in, w_out)


def finish_kernel(
    pick_ref, slots_ref, dwi_in, dwo_in, mixed_out, d_tok_out, dwi_out, dwo_out, spot, sem
):
    moves = []
    for src, dst, n in ((dwi_in, dwi_out, 256), (dwo_in, dwo_out, 512)):
        for j in range(4):
            here = pl.ds(n * j, n)
            d = pltpu.make_async_copy(src.at[here], dst.at[here], sem.at[len(moves)])
            d.start()
            moves.append(d)
    for t, out in enumerate((mixed_out, d_tok_out)):
        spot[t] = dot(pick_ref[...], slots_ref[t], TN).astype(BF)
        d = pltpu.make_async_copy(spot.at[t], out, sem.at[len(moves)])
        d.start()
        moves.append(d)
    for d in moves:
        d.wait()


def finish(pick, slots, d_w_in, d_w_out):
    vmem = pl.BlockSpec(memory_space=pltpu.VMEM)
    anywhere = pl.BlockSpec(memory_space=pl.ANY)
    hbm = pl.BlockSpec(memory_space=pltpu.HBM)
    return pl.pallas_call(
        finish_kernel,
        out_shape=(
            jax.ShapeDtypeStruct((256, 1024), BF),
            jax.ShapeDtypeStruct((256, 1024), BF),
            jax.ShapeDtypeStruct((1024, 2048), BF),
            jax.ShapeDtypeStruct((2048, 1024), BF),
        ),
        in_specs=[vmem, vmem, anywhere, anywhere],
        out_specs=(hbm, hbm, hbm, hbm),
        scratch_shapes=[pltpu.VMEM((2, 256, 1024), BF), pltpu.SemaphoreType.DMA((10,))],
        compiler_params=pltpu.CompilerParams(vmem_limit_bytes=8 * 2**20),
        cost_estimate=pl.CostEstimate(
            flops=6 * 10**7, bytes_accessed=18 * 2**20, transcendentals=0
        ),
    )(pick, slots, d_w_in, d_w_out)


def local(tokens, w_in, w_out, chosen, counts, gates, cotangent):
    return finish(*exchange(chosen, gates, counts.reshape(1, 1), tokens, cotangent, w_in, w_out))


def solution(mesh):
    in_specs = (
        P("dp", "expert"),
        P("expert", "dp"),
        P("dp", "expert"),
        P("dp", None),
        P("dp"),
        P("dp", None),
        P("dp", "expert"),
    )
    out_specs = (P("dp", "expert"), P("dp", "expert"), P("expert", "dp"), P("dp", "expert"))
    return jax.shard_map(local, mesh=mesh, in_specs=in_specs, out_specs=out_specs, check_vma=False)
```
